32 devices in a mesh: bin: 8 (over y, x, core), coil: 4 (over z).
Axes of the slice: x: 2, y: 2, z: 4, core: 2. Of those that a mesh axis runs over, the one named last changes fastest.
Arguments:
- cine_image: bfloat16 [8, 256, 8, 256], P('bin', 'coil'), may hold values from -6 to 6
- warp_blocks: bfloat16 [8, 4096, 2, 4096], P('bin', 'coil'), may hold values from -0.5 to 0.5
- warp_index: int32 [8, 4096, 2], P('bin', 'coil'), may hold values from 0 to 4095, as said below
- sample_mask: int32 [8, 256, 128], P('bin'), may hold values 0 or 1
- kspace_data: bfloat16 [8, 8, 256, 8, 256], P('bin', 'coil'), may hold values from -6 to 6
- sensitivity: bfloat16 [8, 256, 8, 256], P(None, 'coil'), may hold values from -1.5 to 1.5
Outputs:
- gradient: float32 [8, 256, 8, 256], P('bin', 'coil')
The draws below stay inside these ranges and needn't reach their ends.
Inputs may be any that keep to these rules, and one draw needn't show every extreme that they name: `warp_index`: slot 0 of every block names the block itself; every other slot of the block at row y names a block whose row lies among the 16 rows from 16 * (y // 16) on.
All inputs are finite; a program needn't handle non-finite values. No bound on the sum of `sample_mask` on one device may be relied on, other than what follows from the above.
Results may differ from the reference program's by a relative error of at most 0.017.
Values may be sent and summed in bfloat16 or wider, within the bound.
A program may use at most 128 MiB of HBM per device.

```python
import jax
import jax.numpy as jnp
from jax import lax

NY = 256
NX = 128
Z = 8
BLOCK = 64
K = 2
BAND = 16
BINS = 8
COILS = 8
NBLK = 4096


def draw_warp_index(key, part):
    strips = NX // BLOCK
    block_total = NY * Z * strips
    serial = jnp.arange(block_total, dtype=jnp.int32)
    row_number = serial // (Z * strips)
    band_start = row_number // BAND * BAND
    key_row, key_depth, key_strip = jax.random.split(key, 3)
    draw_shape = (BINS, block_total, K - 1)
    row_choice = band_start[None, :, None] + jax.random.randint(key_row, draw_shape, 0, BAND, dtype=jnp.int32)
    depth_choice = jax.random.randint(key_depth, draw_shape, 0, Z, dtype=jnp.int32)
    strip_choice = jax.random.randint(key_strip, draw_shape, 0, strips, dtype=jnp.int32)
    others = (row_choice * Z + depth_choice) * strips + strip_choice
    own_slot = jnp.broadcast_to(serial[None, :, None], (BINS, block_total, 1))
    return jnp.concatenate([own_slot, others], axis=2).astype(jnp.int32)


def place_ends(drawn, key, smallest, largest):
    longest = drawn.shape.index(max(drawn.shape))
    spots = []
    for shift in (0, 1):
        where = [jax.random.randint(jax.random.fold_in(key, axis), (), 0, length) for axis, length in enumerate(drawn.shape)]
        where[longest] = (where[longest] + shift) % drawn.shape[longest]
        spots.append(tuple(where))
    return drawn.at[spots[0]].set(smallest).at[spots[1]].set(largest)


def block_levels(key, extent, shards, smallest, high):
    level, own = 1.0, jax.random.fold_in(key, 6)
    for dim, blocks in shards:
        steps = jnp.exp(jax.random.uniform(jax.random.fold_in(own, dim), (blocks,), jnp.float32, smallest / len(shards), high / len(shards)))
        level = level * jnp.repeat(steps, extent[dim] // blocks).reshape([-1 if axis == dim else 1 for axis in range(len(extent))])
    return level


def noise(stream_key, dims, scale, bound, cuts=(), kind=jnp.bfloat16):
    values = scale * jax.random.normal(stream_key, dims, jnp.float32)
    if cuts:
        values = values * block_levels(stream_key, dims, cuts, -0.22, 0.18)
    return jnp.clip(values, -bound, bound).astype(kind)


def setup_inputs(seed: int = 0) -> dict:
    streams_of = jax.random.split(jax.random.key(seed), 7)
    return {
        "cine_image": noise(streams_of[0], (BINS, NY, Z, 2 * NX), 1.0, 6.0, ((0, 8), (1, 4))),
        "warp_blocks": noise(streams_of[1], (BINS, NBLK, K, BLOCK * BLOCK), (K * BLOCK) ** -0.5, 0.5, ((0, 8), (1, 4))),
        "warp_index": draw_warp_index(jax.random.fold_in(streams_of[6], 71), 0),
        "sample_mask": place_ends((jax.random.randint(streams_of[3], (BINS, NY, NX), 0, 3) < 1).astype(jnp.int32), jax.random.fold_in(streams_of[3], 1), 0, 1),
        "kspace_data": noise(streams_of[4], (BINS, COILS, NY, Z, 2 * NX), 1.0, 6.0, ((0, 8), (1, 4))),
        "sensitivity": noise(streams_of[5], (COILS, NY, Z, 2 * NX), 0.25, 1.5, ((1, 4),)),
    }


def cosine_sine(length):
    positions = jnp.arange(length, dtype=jnp.int32)
    phases = positions[:, None] * positions[None, :] % length
    angles = phases.astype(jnp.float32) * (2.0 * jnp.pi / length)
    factor = 1.0 / jnp.sqrt(jnp.asarray(length, jnp.float32))
    return (jnp.cos(angles) * factor, jnp.sin(angles) * factor)

def make_row_matrix(length):
    cosine_table, sine_table = cosine_sine(length)
    upper_half = jnp.concatenate([cosine_table, -sine_table], axis=1)
    lower_half = jnp.concatenate([sine_table, cosine_table], axis=1)
    return jnp.concatenate([upper_half, lower_half], axis=0).astype(jnp.bfloat16)

def make_column_tables(length):
    cosine_table, sine_table = cosine_sine(length)
    return jnp.stack([cosine_table, sine_table]).astype(jnp.bfloat16)

def row_apply(values, row_matrix, inverse):
    flattened = values.reshape(-1, values.shape[-1])
    table_used = row_matrix.T if inverse else row_matrix
    return jnp.dot(flattened, table_used, preferred_element_type=jnp.float32).reshape(values.shape)

def column_transform(values, tables, inverse):
    products = jnp.einsum('tky,cyzx->tckzx', tables.astype(jnp.float32), values.astype(jnp.float32))
    direct, turned = (products[0], products[1])
    half_width = direct.shape[-1] // 2
    if inverse:
        swapped = jnp.concatenate([-turned[..., half_width:], turned[..., :half_width]], axis=-1)
    else:
        swapped = jnp.concatenate([turned[..., half_width:], -turned[..., :half_width]], axis=-1)
    return direct + swapped

def coil_images(sensitivity, moved_image):
    half_width = moved_image.shape[-1] // 2
    sens_re = sensitivity[..., :half_width].astype(jnp.float32)
    sens_im = sensitivity[..., half_width:].astype(jnp.float32)
    image_re = moved_image[..., :half_width].astype(jnp.float32)
    image_im = moved_image[..., half_width:].astype(jnp.float32)
    real_part = sens_re * image_re - sens_im * image_im
    imag_part = sens_re * image_im + sens_im * image_re
    return jnp.concatenate([real_part, imag_part], axis=-1).astype(jnp.bfloat16)

def conj_sum(sensitivity, back_rows):
    half_width = back_rows.shape[-1] // 2
    sens_re = sensitivity[..., :half_width].astype(jnp.float32)
    sens_im = sensitivity[..., half_width:].astype(jnp.float32)
    back_re = back_rows[..., :half_width]
    back_im = back_rows[..., half_width:]
    real_part = lax.optimization_barrier(jnp.sum(sens_re * back_re + sens_im * back_im, axis=0))
    imag_part = lax.optimization_barrier(jnp.sum(sens_re * back_im - sens_im * back_re, axis=0))
    return jnp.concatenate([real_part, imag_part], axis=-1)

def split_blocks(values):
    row_count, depth_count, full_width = values.shape
    grouped = values.reshape(row_count, depth_count, 2, full_width // (2 * BLOCK), BLOCK)
    return grouped.transpose(0, 1, 3, 2, 4).reshape(-1, 2, BLOCK)

def join_blocks(pieces, row_count, depth_count, full_width):
    grouped = pieces.reshape(row_count, depth_count, full_width // (2 * BLOCK), 2, BLOCK)
    return grouped.transpose(0, 1, 3, 2, 4).reshape(row_count, depth_count, full_width)

def warp_forward(source, weights, block_index):
    pieces = split_blocks(source)
    chosen = jnp.take(pieces, block_index, axis=0)
    matrices = weights.reshape(weights.shape[0], weights.shape[1], BLOCK, BLOCK)
    return jnp.einsum('ikpq,ikcq->icp', matrices.astype(jnp.float32), chosen.astype(jnp.float32))

def warp_adjoint(values, weights, block_index):
    matrices = weights.reshape(weights.shape[0], weights.shape[1], BLOCK, BLOCK)
    contributions = jnp.einsum('ikpq,icp->ikcq', matrices.astype(jnp.float32), values.astype(jnp.float32))
    flattened = contributions.reshape(-1, 2, BLOCK)
    zeros_start = jnp.zeros((values.shape[0], 2, BLOCK), jnp.float32)
    return zeros_start.at[block_index.reshape(-1)].add(flattened)

def reference(cine_image, warp_blocks, warp_index, sample_mask, kspace_data, sensitivity):
    row_matrix = make_row_matrix(NX)
    column_tables = make_column_tables(NY)
    prior_frames = jnp.roll(cine_image, 1, axis=0)

    def forward_bin(operands):
        current, earlier, weights, block_index = operands
        warped = join_blocks(warp_forward(earlier, weights, block_index), NY, Z, 2 * NX)
        return (current.astype(jnp.float32) + warped).astype(jnp.bfloat16)
    moved_image = lax.map(forward_bin, (cine_image, prior_frames, warp_blocks, warp_index))

    def data_bin(operands):
        current, mask_now, measured = operands
        images = coil_images(sensitivity, current)
        row_spectra = row_apply(images, row_matrix, False).astype(jnp.bfloat16)
        spectra = column_transform(row_spectra, column_tables, False)
        weight_mask = jnp.concatenate([mask_now, mask_now], axis=1).astype(jnp.float32)[:, None, :]
        residual = (weight_mask * (spectra - measured.astype(jnp.float32))).astype(jnp.bfloat16)
        back_columns = column_transform(residual, column_tables, True).astype(jnp.bfloat16)
        back_rows = row_apply(back_columns, row_matrix, True)
        return conj_sum(sensitivity, back_rows)
    data_grad = lax.map(data_bin, (moved_image, sample_mask, kspace_data))

    def adjoint_bin(operands):
        grad_now, weights, block_index = operands
        pieces = split_blocks(grad_now.astype(jnp.bfloat16))
        summed = warp_adjoint(pieces, weights, block_index)
        return join_blocks(summed, NY, Z, 2 * NX).astype(jnp.bfloat16)
    pulled = lax.map(adjoint_bin, (data_grad, warp_blocks, warp_index))
    return data_grad + jnp.roll(pulled, -1, axis=0).astype(jnp.float32)
```

```python
import jax
import jax.numpy as jnp
from jax import lax
from jax.experimental import pallas as pl
from jax.experimental.pallas import tpu as pltpu
from jax.sharding import PartitionSpec as P

NY = 256
NX = 128
BLOCK = 64
LANES = 128
ROWS = 128


def shifted(block, axis, distance):
    devices = range(lax.axis_size(axis))
    route = [((i - distance) % len(devices), i) for i in devices]
    return lax.ppermute(block, axis, route)


def cosine_sine(length):
    positions = jnp.arange(length, dtype=jnp.int32)
    phases = positions[:, None] * positions[None, :] % length
    angles = phases.astype(jnp.float32) * (2.0 * jnp.pi / length)
    factor = 1.0 / jnp.sqrt(jnp.asarray(length, jnp.float32))
    return (jnp.cos(angles) * factor, jnp.sin(angles) * factor)


def make_row_matrix(length):
    cosine_table, sine_table = cosine_sine(length)
    upper_half = jnp.concatenate([cosine_table, -sine_table], axis=1)
    lower_half = jnp.concatenate([sine_table, cosine_table], axis=1)
    return jnp.concatenate([upper_half, lower_half], axis=0).astype(jnp.bfloat16)


def make_column_tables(length):
    cosine_table, sine_table = cosine_sine(length)
    return jnp.stack([cosine_table, sine_table]).astype(jnp.bfloat16)


def row_apply(values, row_matrix, inverse):
    flattened = values.reshape(-1, values.shape[-1])
    table_used = row_matrix.T if inverse else row_matrix
    return jnp.dot(flattened, table_used, preferred_element_type=jnp.float32).reshape(values.shape)


def column_transform(values, tables, inverse):
    products = jnp.einsum("tky,cyzx->tckzx", tables, values, preferred_element_type=jnp.float32)
    direct, turned = (products[0], products[1])
    half_width = direct.shape[-1] // 2
    if inverse:
        swapped = jnp.concatenate([-turned[..., half_width:], turned[..., :half_width]], axis=-1)
    else:
        swapped = jnp.concatenate([turned[..., half_width:], -turned[..., :half_width]], axis=-1)
    return direct + swapped


def coil_images(sensitivity, moved_image):
    half_width = moved_image.shape[-1] // 2
    sens_re = sensitivity[..., :half_width].astype(jnp.float32)
    sens_im = sensitivity[..., half_width:].astype(jnp.float32)
    image_re = moved_image[..., :half_width].astype(jnp.float32)
    image_im = moved_image[..., half_width:].astype(jnp.float32)
    real_part = sens_re * image_re - sens_im * image_im
    imag_part = sens_re * image_im + sens_im * image_re
    return jnp.concatenate([real_part, imag_part], axis=-1).astype(jnp.bfloat16)


def conj_sum(sensitivity, back_rows):
    half_width = back_rows.shape[-1] // 2
    sens_re = sensitivity[..., :half_width].astype(jnp.float32)
    sens_im = sensitivity[..., half_width:].astype(jnp.float32)
    back_re = back_rows[..., :half_width]
    back_im = back_rows[..., half_width:]
    real_part = jnp.sum(sens_re * back_re + sens_im * back_im, axis=0)
    imag_part = jnp.sum(sens_re * back_im - sens_im * back_re, axis=0)
    return jnp.concatenate([real_part, imag_part], axis=-1)


def column_part(row_spectra, measured, mask_now, column_tables):
    spectra = column_transform(row_spectra, column_tables, False)
    weight_mask = jnp.concatenate([mask_now, mask_now], axis=1).astype(jnp.float32)[:, None, :]
    residual = (weight_mask * (spectra - measured.astype(jnp.float32))).astype(jnp.bfloat16)
    return column_transform(residual, column_tables, True).astype(jnp.bfloat16)


def one_hot(test):
    return jnp.where(test, 1.0, 0.0).astype(jnp.bfloat16)


def turn(values):
    return pltpu.roll(values, BLOCK, 1)


def strips_to_parts(first, second, low):
    return jnp.where(low, first, turn(second)), jnp.where(low, turn(first), second)


def forward_kernel(w_ref, earlier_ref, current_ref, index_ref, out_ref, source_ref):
    f32, bf16 = jnp.float32, jnp.bfloat16
    rows = ROWS
    low = lax.broadcasted_iota(jnp.int32, (rows, LANES), 1) < BLOCK
    earlier = earlier_ref[...].astype(f32)
    own = (earlier[:, :LANES], earlier[:, LANES:])
    pieces = jnp.concatenate(strips_to_parts(own[0], own[1], low), axis=0).astype(bf16)
    numbers = lax.broadcasted_iota(jnp.int32, (rows, 2 * rows), 1)
    index = index_ref[...]
    chosen = [
        jnp.dot(one_hot(index[:, s : s + 1] == numbers), pieces, preferred_element_type=f32)
        for s in range(2)
    ]
    other = strips_to_parts(chosen[0], chosen[1], low)
    for k, image in enumerate((own, other)):
        for c in range(2):
            plain, turned = image[c], turn(image[c])
            zero = jnp.zeros_like(plain)
            base = k * 4 + c * 2
            source_ref[base, :, :LANES] = jnp.where(low, plain, 0.0)
            source_ref[base + 1, :, :LANES] = jnp.where(low, 0.0, turned)
            source_ref[base + 8, :, LANES:] = jnp.where(low, turned, 0.0)
            source_ref[base + 9, :, LANES:] = jnp.where(low, 0.0, plain)
            for h in range(2):
                source_ref[base + h, :, LANES:] = zero
                source_ref[base + 8 + h, :, :LANES] = zero

    lane = lax.broadcasted_iota(jnp.int32, (BLOCK, LANES), 1)
    row = lax.broadcasted_iota(jnp.int32, (BLOCK, LANES), 0)
    same_slot = row % 2 == lane // 32 % 2
    spot = lane % 8
    er = lax.broadcasted_iota(jnp.int32, (BLOCK, 2 * LANES), 0)
    el = lax.broadcasted_iota(jnp.int32, (BLOCK, 2 * LANES), 1)
    expand = one_hot(el % BLOCK == er // 2 * 2 + el // LANES)
    low8 = low[:8]

    def one_row(y):
        start = pl.multiple_of(y * 8, 8)
        weights = jnp.concatenate(
            [w_ref[pl.ds(start, 8), s].reshape(8 * BLOCK, LANES) for s in range(2)], axis=1
        )
        source = source_ref[:, pl.ds(start, 8), :].reshape(LANES, 2 * LANES).astype(bf16)
        products = lax.dot_general(
            weights, source, (((1,), (1,)), ((), ())), preferred_element_type=f32
        ).reshape(8, BLOCK, LANES)
        kept = products[0]
        for z in range(1, 8):
            kept = jnp.where(spot == z, products[z], kept)
        kept = jnp.where(same_slot, kept, 0.0)
        spread = jnp.dot(kept.T.astype(bf16), expand, preferred_element_type=f32)
        parts = []
        for c in range(2):
            strips = []
            for s in range(2):
                total = None
                for k in range(2):
                    for h in range(2):
                        at = s * 64 + k * 32 + c * 16 + h * 8
                        term = spread[at : at + 8, h * LANES : (h + 1) * LANES]
                        total = term if total is None else total + term
                strips.append(total)
            parts.append(jnp.where(low8, strips[0], strips[1]))
        return jnp.concatenate(parts, axis=1)

    def two_rows(step, carry):
        at = pl.multiple_of(step * 16, 16)
        warped = jnp.concatenate([one_row(step * 2), one_row(step * 2 + 1)], axis=0)
        now = current_ref[pl.ds(at, 16), :].astype(f32)
        out_ref[pl.ds(at, 16), :] = (now + warped).astype(bf16)
        return carry

    lax.fori_loop(0, rows // 16, two_rows, 0)


def adjoint_kernel(w_ref, grad_ref, index_ref, out_ref, spread_ref, own_ref, other_ref):
    f32, bf16 = jnp.float32, jnp.bfloat16
    rows = ROWS
    low = lax.broadcasted_iota(jnp.int32, (rows, LANES), 1) < BLOCK
    grad = grad_ref[...].astype(bf16)
    er = lax.broadcasted_iota(jnp.int32, (LANES, 8 * BLOCK), 0)
    el = lax.broadcasted_iota(jnp.int32, (LANES, 8 * BLOCK), 1)
    for s in range(2):
        for h in range(2):
            expand = one_hot(er == s * BLOCK + el % BLOCK // 2 * 2 + h)
            for c in range(2):
                spread_ref[s * 4 + c * 2 + h] = jnp.dot(
                    grad[:, c * LANES : (c + 1) * LANES], expand, preferred_element_type=f32
                )

    mr = lax.broadcasted_iota(jnp.int32, (8, 8 * BLOCK), 0)
    ml = lax.broadcasted_iota(jnp.int32, (8, 8 * BLOCK), 1)
    masks = [(ml // BLOCK == mr) & (ml % 2 == k) for k in range(2)]
    low8 = low[:8]

    def one_row(y):
        start = pl.multiple_of(y * 8, 8)
        tiles = []
        for s in range(2):
            values = [spread_ref[s * 4 + ch, pl.ds(start, 8), :] for ch in range(4)]
            left = jnp.concatenate(
                [jnp.where(masks[k], values[ch], 0.0) for k in range(2) for ch in range(4)],
                axis=0,
            ).astype(bf16)
            weights = w_ref[pl.ds(start, 8), s].reshape(8 * BLOCK, LANES)
            tiles.append(jnp.dot(left, weights, preferred_element_type=f32))
        for k, ref in enumerate((own_ref, other_ref)):
            for c in range(2):
                at = k * 32 + c * 16
                plain = jnp.where(low8, tiles[0][at : at + 8], tiles[1][at + 8 : at + 16])
                moved = jnp.where(low8, tiles[1][at : at + 8], tiles[0][at + 8 : at + 16])
                ref[c, pl.ds(start, 8), :] = plain + turn(moved)

    def two_rows(step, carry):
        one_row(step * 2)
        one_row(step * 2 + 1)
        return carry

    lax.fori_loop(0, rows // 16, two_rows, 0)
    numbers = lax.broadcasted_iota(jnp.int32, (2 * rows, rows), 0)
    index = index_ref[...]
    select = jnp.concatenate(
        [one_hot(index[s : s + 1, :] == numbers) for s in range(2)], axis=1
    )
    terms = jnp.concatenate(strips_to_parts(other_ref[0], other_ref[1], low), axis=0)
    upper = terms.astype(bf16)
    lower = (terms - upper.astype(f32)).astype(bf16)
    summed = jnp.dot(select, upper, preferred_element_type=f32) + jnp.dot(
        select, lower, preferred_element_type=f32
    )
    parts = strips_to_parts(summed[:rows], summed[rows:], low)
    out_ref[...] = jnp.concatenate(
        [parts[0] + own_ref[0], parts[1] + own_ref[1]], axis=1
    ).astype(bf16)


def band_call(kernel, bands, inputs, specs, scratch, flops, moved):
    return pl.pallas_call(
        kernel,
        grid=(bands,),
        in_specs=specs,
        out_specs=pl.BlockSpec((ROWS, 2 * LANES), lambda b: (b, 0)),
        out_shape=jax.ShapeDtypeStruct((bands * ROWS, 2 * LANES), jnp.bfloat16),
        scratch_shapes=scratch,
        compiler_params=pltpu.CompilerParams(vmem_limit_bytes=40 * 1024 * 1024),
        cost_estimate=pl.CostEstimate(flops=flops, bytes_accessed=moved, transcendentals=0),
    )(*inputs)


def weight_spec():
    return pl.BlockSpec((ROWS, 2, BLOCK, LANES), lambda b: (b, 0, 0, 0))


def image_spec():
    return pl.BlockSpec((ROWS, 2 * LANES), lambda b: (b, 0))


def warp_forward(earlier, current, weights, index_columns):
    bands = earlier.shape[0] // ROWS
    return band_call(
        forward_kernel,
        bands,
        (weights, earlier, current, index_columns),
        [weight_spec(), image_spec(), image_spec(), pl.BlockSpec((ROWS, 2), lambda b: (b, 0))],
        [pltpu.VMEM((16, ROWS, 2 * LANES), jnp.float32)],
        bands * 2**31,
        bands * 2**22,
    )


def warp_adjoint(grad, weights, index_rows):
    bands = grad.shape[0] // ROWS
    return band_call(
        adjoint_kernel,
        bands,
        (weights, grad, index_rows),
        [weight_spec(), image_spec(), pl.BlockSpec((2, ROWS), lambda b: (0, b))],
        [
            pltpu.VMEM((8, ROWS, 8 * BLOCK), jnp.float32),
            pltpu.VMEM((2, ROWS, LANES), jnp.float32),
            pltpu.VMEM((2, ROWS, LANES), jnp.float32),
        ],
        bands * 2**31,
        bands * 2**22,
    )


def arrange_weights(blocks):
    count = blocks.shape[0]
    lines = blocks.reshape(count, 2, BLOCK * BLOCK // LANES, LANES)
    return lines.transpose(0, 2, 1, 3).reshape(count // 2, 2, BLOCK, LANES)


def band_places(block_index):
    in_band = block_index[:, 1] % (2 * ROWS)
    return (in_band % 2 * ROWS + in_band // 2).reshape(-1, 2)


def on_device(cine_image, warp_blocks, warp_index, sample_mask, kspace_data, sensitivity):
    current = cine_image[0]
    row_count, depth_count, full_width = current.shape
    row_matrix = make_row_matrix(NX)
    column_tables = make_column_tables(NY)
    earlier = shifted(cine_image, "bin", 1)[0]
    weights = arrange_weights(warp_blocks[0])
    places = band_places(warp_index[0])
    flat_shape = (row_count * depth_count, full_width)
    moved_image = warp_forward(
        earlier.reshape(flat_shape), current.reshape(flat_shape), weights, places
    ).reshape(current.shape)
    measured = kspace_data[0]
    mask_now = sample_mask[0]
    coil_sens = lax.all_to_all(sensitivity, "coil", split_axis=0, concat_axis=1, tiled=True)
    sens_rows = coil_sens
    images = coil_images(sens_rows, lax.all_gather(moved_image, "coil", axis=0, tiled=True))
    own_coils = row_apply(images, row_matrix, False).astype(jnp.bfloat16)
    back_columns = column_part(own_coils, measured, mask_now, column_tables)
    sens_rows = coil_sens
    data_grad = lax.psum_scatter(
        conj_sum(sens_rows, row_apply(back_columns, row_matrix, True)).astype(jnp.bfloat16),
        "coil",
        scatter_dimension=0,
        tiled=True,
    ).astype(jnp.float32)
    pulled = warp_adjoint(data_grad.reshape(flat_shape), weights, places.T).reshape(current.shape)
    from_next = shifted(pulled, "bin", -1)
    return (data_grad + from_next.astype(jnp.float32))[None]


def solution(mesh):
    return jax.shard_map(
        on_device,
        mesh=mesh,
        in_specs=(
            P("bin", "coil", None, None),
            P("bin", "coil", None, None),
            P("bin", "coil", None),
            P("bin", None, None),
            P("bin", "coil", None, None, None),
            P(None, "coil", None, None),
        ),
        out_specs=P("bin", "coil", None, None),
        check_vma=False,
    )
```

```python
import jax
import jax.numpy as jnp
from jax import lax
from jax.experimental import pallas as pl
from jax.experimental.pallas import tpu as pltpu
from jax.sharding import PartitionSpec as P

NY = 256
NX = 128
BLOCK = 64
LANES = 128
ROWS = 128


def shifted(block, axis, distance):
    devices = range(lax.axis_size(axis))
    route = [((i - distance) % len(devices), i) for i in devices]
    return lax.ppermute(block, axis, route)


def cosine_sine(length):
    positions = jnp.arange(length, dtype=jnp.int32)
    phases = positions[:, None] * positions[None, :] % length
    angles = phases.astype(jnp.float32) * (2.0 * jnp.pi / length)
    factor = 1.0 / jnp.sqrt(jnp.asarray(length, jnp.float32))
    return (jnp.cos(angles) * factor, jnp.sin(angles) * factor)


def make_row_matrix(length):
    cosine_table, sine_table = cosine_sine(length)
    upper_half = jnp.concatenate([cosine_table, -sine_table], axis=1)
    lower_half = jnp.concatenate([sine_table, cosine_table], axis=1)
    return jnp.concatenate([upper_half, lower_half], axis=0).astype(jnp.bfloat16)


def make_column_tables(length):
    cosine_table, sine_table = cosine_sine(length)
    return jnp.stack([cosine_table, sine_table]).astype(jnp.bfloat16)


def halves_swapped(values):
    return jnp.concatenate([values[:, LANES:], values[:, :LANES]], axis=1)


def coil_kernel(
    moved_ref, sens_ref, kspace_ref, mask_ref, row_ref, back_ref, column_ref, out_ref,
    wide_ref, sums_ref, send_ref, recv_ref, send_sem, recv_sem,
):
    f32, bf16 = jnp.float32, jnp.bfloat16
    me, count = lax.axis_index("coil"), lax.axis_size("coil")
    coils, depth = sens_ref.shape[0], sens_ref.shape[1]
    own = NY // count
    meet("coil")
    for part in range(2):
        wide_ref[part] = moved_ref[:, part * LANES : (part + 1) * LANES].astype(f32)

    def multiply(left, right):
        return jnp.dot(left, right, preferred_element_type=f32)

    def transfer(step, z):
        target = lax.rem(me + step, count)
        rows = pl.ds(pl.multiple_of(target * own, own), own)
        return pltpu.make_async_remote_copy(
            src_ref=send_ref.at[z, rows],
            dst_ref=recv_ref.at[step - 1, z],
            send_sem=send_sem.at[step - 1, z],
            recv_sem=recv_sem.at[step - 1, z],
            device_id={"coil": target},
            device_id_type=pl.DeviceIdType.MESH,
        )

    def one_depth(z, carry):
        image_re = wide_ref[0, pl.ds(z, NY, stride=depth), :]
        image_im = wide_ref[1, pl.ds(z, NY, stride=depth), :]
        mask = mask_ref[...].astype(f32)
        mask = jnp.concatenate([mask, mask], axis=1)
        total_re = total_im = 0.0
        for c in range(coils):
            sens = sens_ref[c, z].astype(f32)
            sens_re, sens_im = sens[:, :LANES], sens[:, LANES:]
            coil_image = jnp.concatenate(
                [
                    sens_re * image_re - sens_im * image_im,
                    sens_re * image_im + sens_im * image_re,
                ],
                axis=1,
            ).astype(bf16)
            row_spectra = multiply(coil_image, row_ref[...]).astype(bf16)
            products = multiply(column_ref[...], row_spectra)
            direct, turned = products[:NY], halves_swapped(products[NY:])
            spectra = jnp.concatenate(
                [direct[:, :LANES] + turned[:, :LANES], direct[:, LANES:] - turned[:, LANES:]],
                axis=1,
            )
            residual = (mask * (spectra - kspace_ref[c, z].astype(f32))).astype(bf16)
            products = multiply(column_ref[...], residual)
            direct, turned = products[:NY], halves_swapped(products[NY:])
            columns = jnp.concatenate(
                [direct[:, :LANES] - turned[:, :LANES], direct[:, LANES:] + turned[:, LANES:]],
                axis=1,
            ).astype(bf16)
            back = multiply(columns, back_ref[...])
            back_re, back_im = back[:, :LANES], back[:, LANES:]
            total_re += sens_re * back_re + sens_im * back_im
            total_im += sens_re * back_im - sens_im * back_re
        send_ref[z] = jnp.concatenate([total_re, total_im], axis=1).astype(bf16)
        for step in range(1, count):
            transfer(step, z).start()
        return carry

    def collect(z, carry):
        rows = pl.ds(pl.multiple_of(me * own, own), own)
        total = send_ref[z, rows, :].astype(f32)
        for step in range(1, count):
            transfer(step, z).wait_recv()
            total += recv_ref[step - 1, z].astype(f32)
        for part in range(2):
            sums_ref[part, pl.ds(z, own, stride=depth), :] = total[
                :, part * LANES : (part + 1) * LANES
            ]
        for step in range(1, count):
            transfer(step, z).wait_send()
        return carry

    lax.fori_loop(0, depth, one_depth, 0)
    lax.fori_loop(0, depth, collect, 0)
    out_ref[...] = jnp.concatenate([sums_ref[0], sums_ref[1]], axis=1)


def coil_gradient(moved, sens, kspace, mask, row_matrix, column_tables):
    count = lax.axis_size("coil")
    coils, depth = sens.shape[:2]
    own = NY // count
    vmem = pl.BlockSpec(memory_space=pltpu.VMEM)
    return pl.pallas_call(
        coil_kernel,
        in_specs=[vmem] * 7,
        out_specs=vmem,
        out_shape=jax.ShapeDtypeStruct((own * depth, 2 * LANES), jnp.float32),
        scratch_shapes=[
            pltpu.VMEM((2, NY * depth, LANES), jnp.float32),
            pltpu.VMEM((2, own * depth, LANES), jnp.float32),
            pltpu.VMEM((depth, NY, 2 * LANES), jnp.bfloat16),
            pltpu.VMEM((count - 1, depth, own, 2 * LANES), jnp.bfloat16),
            pltpu.SemaphoreType.DMA((count - 1, depth)),
            pltpu.SemaphoreType.DMA((count - 1, depth)),
        ],
        compiler_params=pltpu.CompilerParams(
            collective_id=1, has_side_effects=True, vmem_limit_bytes=40 * 1024 * 1024
        ),
        cost_estimate=pl.CostEstimate(
            flops=coils * 2**31, bytes_accessed=coils * 2**22, transcendentals=0
        ),
    )(moved, sens, kspace, mask, row_matrix, row_matrix.T, column_tables)


def own_coil_maps(sensitivity):
    coils, row_count, depth, width = sensitivity.shape
    bins, count = lax.axis_size("bin"), lax.axis_size("coil")
    share = row_count // bins
    mine = lax.dynamic_slice_in_dim(sensitivity, lax.axis_index("bin") * share, share, axis=1)
    swapped = lax.all_to_all(mine, "coil", split_axis=0, concat_axis=1, tiled=True)
    full = lax.all_gather(swapped, "bin", axis=0, tiled=False)
    full = full.reshape(bins, coils // count, count, share, depth, width)
    return full.transpose(1, 4, 2, 0, 3, 5).reshape(coils // count, depth, NY, width)


def one_hot(test):
    return jnp.where(test, 1.0, 0.0).astype(jnp.bfloat16)


def turn(values):
    return pltpu.roll(values, BLOCK, 1)


def strips_to_parts(first, second, low):
    return jnp.where(low, first, turn(second)), jnp.where(low, turn(first), second)


def meet(axis):
    me, count = lax.axis_index(axis), lax.axis_size(axis)
    barrier = pltpu.get_barrier_semaphore()
    for step in range(1, count):
        pl.semaphore_signal(
            barrier,
            inc=1,
            device_id={axis: lax.rem(me + step, count)},
            device_id_type=pl.DeviceIdType.MESH,
        )
    pl.semaphore_wait(barrier, count - 1)


def forward_kernel(
    w_hbm, earlier_ref, current_ref, index_ref, out_ref, w_buffer, source_ref,
    load_sem, send_sem, recv_sem,
):
    me, count = lax.axis_index("coil"), lax.axis_size("coil")
    total_rows = current_ref.shape[0]
    bands = total_rows // ROWS
    first_row = me * total_rows

    def load(b):
        return pltpu.make_async_copy(
            w_hbm.at[pl.ds(b * ROWS, ROWS)], w_buffer.at[b % 2], load_sem.at[b % 2]
        )

    load(0).start()
    meet("coil")
    sends = []
    for b in range(bands):
        load(b).wait()
        if b + 1 < bands:
            load(b + 1).start()
        part = pl.ds(b * ROWS, ROWS)
        place = pl.ds(pl.multiple_of(first_row + b * ROWS, ROWS), ROWS)
        forward_band(
            w_buffer.at[b % 2],
            earlier_ref.at[part],
            current_ref.at[part],
            index_ref.at[part],
            out_ref.at[place],
            source_ref,
        )
        for step in range(1, count):
            copy = pltpu.make_async_remote_copy(
                src_ref=out_ref.at[place],
                dst_ref=out_ref.at[place],
                send_sem=send_sem.at[b, step - 1],
                recv_sem=recv_sem.at[b, step - 1],
                device_id={"coil": lax.rem(me + step, count)},
                device_id_type=pl.DeviceIdType.MESH,
            )
            copy.start()
            sends.append(copy)
    for copy in sends:
        copy.wait()


def forward_band(w_ref, earlier_ref, current_ref, index_ref, out_ref, source_ref):
    f32, bf16 = jnp.float32, jnp.bfloat16
    rows = ROWS
    low = lax.broadcasted_iota(jnp.int32, (rows, LANES), 1) < BLOCK
    earlier = earlier_ref[...].astype(f32)
    own = (earlier[:, :LANES], earlier[:, LANES:])
    pieces = jnp.concatenate(strips_to_parts(own[0], own[1], low), axis=0).astype(bf16)
    numbers = lax.broadcasted_iota(jnp.int32, (rows, 2 * rows), 1)
    index = index_ref[...]
    chosen = [
        jnp.dot(one_hot(index[:, s : s + 1] == numbers), pieces, preferred_element_type=f32)
        for s in range(2)
    ]
    other = strips_to_parts(chosen[0], chosen[1], low)
    for k, image in enumerate((own, other)):
        for c in range(2):
            plain, turned = image[c], turn(image[c])
            zero = jnp.zeros_like(plain)
            base = k * 8 + c * 2
            source_ref[base, :, :LANES] = jnp.where(low, plain, 0.0)
            source_ref[base + 1, :, :LANES] = jnp.where(low, 0.0, turned)
            source_ref[base + 4, :, LANES:] = jnp.where(low, turned, 0.0)
            source_ref[base + 5, :, LANES:] = jnp.where(low, 0.0, plain)
            for h in range(2):
                source_ref[base + h, :, LANES:] = zero
                source_ref[base + 4 + h, :, :LANES] = zero

    lane = lax.broadcasted_iota(jnp.int32, (BLOCK, LANES), 1)
    row = lax.broadcasted_iota(jnp.int32, (BLOCK, LANES), 0)
    same_slot = row % 2 == lane // 64
    spot = lane % 8
    er = lax.broadcasted_iota(jnp.int32, (BLOCK, 2 * LANES), 0)
    el = lax.broadcasted_iota(jnp.int32, (BLOCK, 2 * LANES), 1)
    expand = one_hot(el % BLOCK == er // 2 * 2 + el // LANES)
    low8 = low[:8]

    def one_row(y):
        start = pl.multiple_of(y * 8, 8)
        weights = jnp.concatenate(
            [w_ref[pl.ds(start, 8), s].reshape(8 * BLOCK, LANES) for s in range(2)], axis=1
        )
        source = source_ref[:, pl.ds(start, 8), :].reshape(LANES, 2 * LANES).astype(bf16)
        products = lax.dot_general(
            weights, source, (((1,), (1,)), ((), ())), preferred_element_type=f32
        ).reshape(8, BLOCK, LANES)
        kept = products[0]
        for z in range(1, 8):
            kept = jnp.where(spot == z, products[z], kept)
        kept = jnp.where(same_slot, kept, 0.0)
        return kept + turn(kept)

    def two_rows(step):
        at = pl.multiple_of(step * 16, 16)
        pair = jnp.where(lane < BLOCK, one_row(step * 2), one_row(step * 2 + 1))
        spread = jnp.dot(pair.T.astype(bf16), expand, preferred_element_type=f32)
        lines = []
        for y in range(2):
            parts = []
            for c in range(2):
                strips = []
                for s in range(2):
                    i = y * 64 + s * 32 + c * 16
                    strips.append(spread[i : i + 8, :LANES] + spread[i + 8 : i + 16, LANES:])
                parts.append(jnp.where(low8, strips[0], strips[1]))
            lines.append(jnp.concatenate(parts, axis=1))
        warped = jnp.concatenate(lines, axis=0)
        now = current_ref[pl.ds(at, 16), :].astype(f32)
        out_ref[pl.ds(at, 16), :] = (now + warped).astype(bf16)

    def four_rows(step, carry):
        two_rows(step * 2)
        two_rows(step * 2 + 1)
        return carry

    lax.fori_loop(0, rows // 32, four_rows, 0)


def adjoint_kernel(w_ref, grad_ref, index_ref, out_ref, spread_ref, own_ref, other_ref):
    f32, bf16 = jnp.float32, jnp.bfloat16
    rows = ROWS
    low = lax.broadcasted_iota(jnp.int32, (rows, LANES), 1) < BLOCK
    grad = grad_ref[...].astype(bf16)
    er = lax.broadcasted_iota(jnp.int32, (LANES, 8 * BLOCK), 0)
    el = lax.broadcasted_iota(jnp.int32, (LANES, 8 * BLOCK), 1)
    for s in range(2):
        for h in range(2):
            expand = one_hot(er == s * BLOCK + el % BLOCK // 2 * 2 + h)
            for c in range(2):
                spread_ref[s * 4 + c * 2 + h] = jnp.dot(
                    grad[:, c * LANES : (c + 1) * LANES], expand, preferred_element_type=f32
                )

    mr = lax.broadcasted_iota(jnp.int32, (8, 8 * BLOCK), 0)
    ml = lax.broadcasted_iota(jnp.int32, (8, 8 * BLOCK), 1)
    masks = [(ml // BLOCK == mr) & (ml % 2 == k) for k in range(2)]
    low8 = low[:8]

    def one_row(y):
        start = pl.multiple_of(y * 8, 8)
        tiles = []
        for s in range(2):
            values = [spread_ref[s * 4 + ch, pl.ds(start, 8), :] for ch in range(4)]
            left = jnp.concatenate(
                [jnp.where(masks[k], values[ch], 0.0) for k in range(2) for ch in range(4)],
                axis=0,
            ).astype(bf16)
            weights = w_ref[pl.ds(start, 8), s].reshape(8 * BLOCK, LANES)
            tiles.append(jnp.dot(left, weights, preferred_element_type=f32))
        for k, ref in enumerate((own_ref, other_ref)):
            for c in range(2):
                at = k * 32 + c * 16
                plain = jnp.where(low8, tiles[0][at : at + 8], tiles[1][at + 8 : at + 16])
                moved = jnp.where(low8, tiles[1][at : at + 8], tiles[0][at + 8 : at + 16])
                ref[c, pl.ds(start, 8), :] = plain + turn(moved)

    def two_rows(step, carry):
        one_row(step * 2)
        one_row(step * 2 + 1)
        return carry

    lax.fori_loop(0, rows // 16, two_rows, 0)
    numbers = lax.broadcasted_iota(jnp.int32, (2 * rows, rows), 0)
    index = index_ref[...]
    select = jnp.concatenate(
        [one_hot(index[s : s + 1, :] == numbers) for s in range(2)], axis=1
    )
    terms = jnp.concatenate(strips_to_parts(other_ref[0], other_ref[1], low), axis=0)
    upper = terms.astype(bf16)
    lower = (terms - upper.astype(f32)).astype(bf16)
    summed = jnp.dot(select, upper, preferred_element_type=f32) + jnp.dot(
        select, lower, preferred_element_type=f32
    )
    parts = strips_to_parts(summed[:rows], summed[rows:], low)
    out_ref[...] = jnp.concatenate(
        [parts[0] + own_ref[0], parts[1] + own_ref[1]], axis=1
    ).astype(bf16)


def band_call(kernel, bands, inputs, specs, scratch, flops, moved):
    return pl.pallas_call(
        kernel,
        grid=(bands,),
        in_specs=specs,
        out_specs=pl.BlockSpec((ROWS, 2 * LANES), lambda b: (b, 0)),
        out_shape=jax.ShapeDtypeStruct((bands * ROWS, 2 * LANES), jnp.bfloat16),
        scratch_shapes=scratch,
        compiler_params=pltpu.CompilerParams(vmem_limit_bytes=40 * 1024 * 1024),
        cost_estimate=pl.CostEstimate(flops=flops, bytes_accessed=moved, transcendentals=0),
    )(*inputs)


def weight_spec():
    return pl.BlockSpec((ROWS, 2, BLOCK, LANES), lambda b: (b, 0, 0, 0))


def image_spec():
    return pl.BlockSpec((ROWS, 2 * LANES), lambda b: (b, 0))


def warp_forward(earlier, current, weights, index_columns):
    count = lax.axis_size("coil")
    rows = earlier.shape[0]
    bands = rows // ROWS
    vmem = pl.BlockSpec(memory_space=pltpu.VMEM)
    return pl.pallas_call(
        forward_kernel,
        in_specs=[pl.BlockSpec(memory_space=pl.ANY), vmem, vmem, vmem],
        out_specs=vmem,
        out_shape=jax.ShapeDtypeStruct((count * rows, 2 * LANES), jnp.bfloat16),
        scratch_shapes=[
            pltpu.VMEM((2, ROWS, 2, BLOCK, LANES), jnp.bfloat16),
            pltpu.VMEM((16, ROWS, 2 * LANES), jnp.float32),
            pltpu.SemaphoreType.DMA((2,)),
            pltpu.SemaphoreType.DMA((bands, count - 1)),
            pltpu.SemaphoreType.DMA((bands, count - 1)),
        ],
        compiler_params=pltpu.CompilerParams(
            collective_id=0, has_side_effects=True, vmem_limit_bytes=40 * 1024 * 1024
        ),
        cost_estimate=pl.CostEstimate(
            flops=bands * 2**31, bytes_accessed=bands * 2**22, transcendentals=0
        ),
    )(weights, earlier, current, index_columns)


def warp_adjoint(grad, weights, index_rows):
    bands = grad.shape[0] // ROWS
    return band_call(
        adjoint_kernel,
        bands,
        (weights, grad, index_rows),
        [weight_spec(), image_spec(), pl.BlockSpec((2, ROWS), lambda b: (0, b))],
        [
            pltpu.VMEM((8, ROWS, 8 * BLOCK), jnp.float32),
            pltpu.VMEM((2, ROWS, LANES), jnp.float32),
            pltpu.VMEM((2, ROWS, LANES), jnp.float32),
        ],
        bands * 2**31,
        bands * 2**22,
    )


def arrange_weights(blocks):
    count = blocks.shape[0]
    lines = blocks.reshape(count, 2, BLOCK * BLOCK // LANES, LANES)
    return lines.transpose(0, 2, 1, 3).reshape(count // 2, 2, BLOCK, LANES)


def band_places(block_index):
    in_band = block_index[:, 1] % (2 * ROWS)
    return (in_band % 2 * ROWS + in_band // 2).reshape(-1, 2)


def on_device(cine_image, warp_blocks, warp_index, sample_mask, kspace_data, sensitivity):
    current = cine_image[0]
    row_count, depth_count, full_width = current.shape
    row_matrix = make_row_matrix(NX)
    column_tables = make_column_tables(NY).reshape(2 * NY, NY)
    earlier = shifted(cine_image, "bin", 1)[0]
    sens = own_coil_maps(sensitivity)
    kspace = kspace_data[0].transpose(0, 2, 1, 3)
    weights = arrange_weights(warp_blocks[0])
    places = band_places(warp_index[0])
    flat_shape = (row_count * depth_count, full_width)
    moved_image = warp_forward(
        earlier.reshape(flat_shape), current.reshape(flat_shape), weights, places
    )
    data_grad = coil_gradient(
        moved_image, sens, kspace, sample_mask[0], row_matrix, column_tables
    )
    pulled = warp_adjoint(data_grad, weights, places.T).reshape(current.shape)
    from_next = shifted(pulled, "bin", -1)
    return (data_grad.reshape(current.shape) + from_next.astype(jnp.float32))[None]


def solution(mesh):
    return jax.shard_map(
        on_device,
        mesh=mesh,
        in_specs=(
            P("bin", "coil", None, None),
            P("bin", "coil", None, None),
            P("bin", "coil", None),
            P("bin", None, None),
            P("bin", "coil", None, None, None),
            P(None, "coil", None, None),
        ),
        out_specs=P("bin", "coil", None, None),
        check_vma=False,
    )
```

```python
import jax
import jax.numpy as jnp
from jax import lax
from jax.experimental import pallas as pl
from jax.experimental.pallas import tpu as pltpu
from jax.sharding import PartitionSpec as P

NY = 256
NX = 128
BLOCK = 64
LANES = 128
ROWS = 128
LAG = 2


def shifted(block, axis, distance):
    devices = range(lax.axis_size(axis))
    route = [((i - distance) % len(devices), i) for i in devices]
    return lax.ppermute(block, axis, route)


def cosine_sine(length):
    positions = jnp.arange(length, dtype=jnp.int32)
    phases = positions[:, None] * positions[None, :] % length
    angles = phases.astype(jnp.float32) * (2.0 * jnp.pi / length)
    factor = 1.0 / jnp.sqrt(jnp.asarray(length, jnp.float32))
    return (jnp.cos(angles) * factor, jnp.sin(angles) * factor)


def make_row_matrix(length):
    cosine_table, sine_table = cosine_sine(length)
    upper_half = jnp.concatenate([cosine_table, -sine_table], axis=1)
    lower_half = jnp.concatenate([sine_table, cosine_table], axis=1)
    return jnp.concatenate([upper_half, lower_half], axis=0).astype(jnp.bfloat16)


def make_column_tables(length):
    cosine_table, sine_table = cosine_sine(length)
    return jnp.stack([cosine_table, sine_table]).astype(jnp.bfloat16)


def halves_swapped(values):
    return jnp.concatenate([values[:, LANES:], values[:, :LANES]], axis=1)


def coil_kernel(
    moved_ref, sens_ref, kspace_ref, mask_ref, row_ref, back_ref, column_ref, index_ref, w_hbm,
    out_ref, pulled_ref,
    wide_ref, sums_ref, send_ref, recv_ref, w_ref, expand_ref, spread_ref, warp_ref,
    send_sem, recv_sem, load_sem,
):
    f32, bf16 = jnp.float32, jnp.bfloat16
    me, count = lax.axis_index("coil"), lax.axis_size("coil")
    coils, depth = sens_ref.shape[0], sens_ref.shape[1]
    own = NY // count
    load = pltpu.make_async_copy(w_hbm, w_ref, load_sem)
    load.start()
    meet("coil")
    er = lax.broadcasted_iota(jnp.int32, (LANES, 8 * BLOCK), 0)
    el = lax.broadcasted_iota(jnp.int32, (LANES, 8 * BLOCK), 1)
    for s in range(2):
        for h in range(2):
            expand_ref[s * 2 + h] = one_hot(er == s * BLOCK + el % BLOCK // 2 * 2 + h)
    mr = lax.broadcasted_iota(jnp.int32, (8, 8 * BLOCK), 0)
    ml = lax.broadcasted_iota(jnp.int32, (8, 8 * BLOCK), 1)
    masks = [(ml // BLOCK == mr) & (ml % 2 == k) for k in range(2)]
    low = lax.broadcasted_iota(jnp.int32, (ROWS, LANES), 1) < BLOCK
    low8 = low[:8]
    for part in range(2):
        wide_ref[part] = moved_ref[:, part * LANES : (part + 1) * LANES].astype(f32)

    def multiply(left, right):
        return jnp.dot(left, right, preferred_element_type=f32)

    def transfer(step, z):
        target = lax.rem(me + step, count)
        rows = pl.ds(pl.multiple_of(target * own, own), own)
        return pltpu.make_async_remote_copy(
            src_ref=send_ref.at[z, rows],
            dst_ref=recv_ref.at[step - 1, z],
            send_sem=send_sem.at[step - 1, z],
            recv_sem=recv_sem.at[step - 1, z],
            device_id={"coil": target},
            device_id_type=pl.DeviceIdType.MESH,
        )

    def one_depth(z):
        image_re = wide_ref[0, pl.ds(z, NY, stride=depth), :]
        image_im = wide_ref[1, pl.ds(z, NY, stride=depth), :]
        mask = mask_ref[...].astype(f32)
        mask = jnp.concatenate([mask, mask], axis=1)
        total_re = total_im = 0.0
        for c in range(coils):
            sens = jnp.concatenate(
                [sens_ref[c, z, lax.rem(me - w + count, count)] for w in range(count)], axis=0
            ).astype(f32)
            sens_re, sens_im = sens[:, :LANES], sens[:, LANES:]
            coil_image = jnp.concatenate(
                [
                    sens_re * image_re - sens_im * image_im,
                    sens_re * image_im + sens_im * image_re,
                ],
                axis=1,
            ).astype(bf16)
            row_spectra = multiply(coil_image, row_ref[...]).astype(bf16)
            products = multiply(column_ref[...], row_spectra)
            direct, turned = products[:NY], halves_swapped(products[NY:])
            spectra = jnp.concatenate(
                [direct[:, :LANES] + turned[:, :LANES], direct[:, LANES:] - turned[:, LANES:]],
                axis=1,
            )
            residual = (mask * (spectra - kspace_ref[c, z].astype(f32))).astype(bf16)
            products = multiply(column_ref[...], residual)
            direct, turned = products[:NY], halves_swapped(products[NY:])
            columns = jnp.concatenate(
                [direct[:, :LANES] - turned[:, :LANES], direct[:, LANES:] + turned[:, LANES:]],
                axis=1,
            ).astype(bf16)
            back = multiply(columns, back_ref[...])
            back_re, back_im = back[:, :LANES], back[:, LANES:]
            total_re += sens_re * back_re + sens_im * back_im
            total_im += sens_re * back_im - sens_im * back_re
        send_ref[z] = jnp.concatenate([total_re, total_im], axis=1).astype(bf16)
        for step in range(1, count):
            transfer(step, z).start()

    def adjoint_depth(z):
        rows = pl.ds(pl.multiple_of(me * own, own), own)
        total = send_ref[z, rows, :].astype(f32)
        for step in range(1, count):
            transfer(step, z).wait_recv()
            total += recv_ref[step - 1, z].astype(f32)
        for part in range(2):
            sums_ref[part, pl.ds(z, own, stride=depth), :] = total[
                :, part * LANES : (part + 1) * LANES
            ]
        grad = total.astype(bf16)
        for s in range(2):
            for h in range(2):
                for c in range(2):
                    spread_ref[s * 4 + c * 2 + h] = multiply(
                        grad[:, c * LANES : (c + 1) * LANES], expand_ref[s * 2 + h]
                    )

        def one_group(q):
            start = pl.multiple_of(q * 8, 8)
            tiles = []
            for s in range(2):
                values = [spread_ref[s * 4 + ch, pl.ds(start, 8), :] for ch in range(4)]
                left = jnp.concatenate(
                    [jnp.where(masks[k], values[ch], 0.0) for k in range(2) for ch in range(4)],
                    axis=0,
                ).astype(bf16)
                weights = w_ref[pl.ds(start, 8), z, s].reshape(8 * BLOCK, LANES)
                tiles.append(multiply(left, weights))
            for k in range(2):
                for c in range(2):
                    at = k * 32 + c * 16
                    plain = jnp.where(low8, tiles[0][at : at + 8], tiles[1][at + 8 : at + 16])
                    moved = jnp.where(low8, tiles[1][at : at + 8], tiles[0][at + 8 : at + 16])
                    place = pl.ds(start * depth + z, 8, stride=depth)
                    warp_ref[k * 2 + c, place, :] = plain + turn(moved)

        def two_groups(step, carry):
            one_group(step * 2)
            one_group(step * 2 + 1)
            return carry

        lax.fori_loop(0, own // 16, two_groups, 0)

    def forward_step(z, carry):
        one_depth(z)

        @pl.when(z >= LAG)
        def _():
            @pl.when(z == LAG)
            def _():
                load.wait()

            adjoint_depth(z - LAG)

        return carry

    def last_step(z, carry):
        adjoint_depth(z)
        return carry

    def sent(z, carry):
        for step in range(1, count):
            transfer(step, z).wait_send()
        return carry

    lax.fori_loop(0, depth, forward_step, 0)
    lax.fori_loop(depth - LAG, depth, last_step, 0)
    out_ref[...] = jnp.concatenate([sums_ref[0], sums_ref[1]], axis=1)
    numbers = lax.broadcasted_iota(jnp.int32, (2 * ROWS, ROWS), 0)
    for band in range(own * depth // ROWS):
        part = pl.ds(band * ROWS, ROWS)
        index = index_ref[:, part]
        select = jnp.concatenate(
            [one_hot(index[s : s + 1, :] == numbers) for s in range(2)], axis=1
        )
        terms = jnp.concatenate(
            strips_to_parts(warp_ref[2, part, :], warp_ref[3, part, :], low), axis=0
        )
        upper = terms.astype(bf16)
        lower = (terms - upper.astype(f32)).astype(bf16)
        summed = multiply(select, upper) + multiply(select, lower)
        parts = strips_to_parts(summed[:ROWS], summed[ROWS:], low)
        pulled_ref[part, :] = jnp.concatenate(
            [parts[0] + warp_ref[0, part, :], parts[1] + warp_ref[1, part, :]], axis=1
        ).astype(bf16)
    lax.fori_loop(0, depth, sent, 0)


def coil_gradient(
    moved, sens, kspace, mask, row_matrix, column_tables, index_rows, weights
):
    count = lax.axis_size("coil")
    coils, depth = sens.shape[:2]
    own = NY // count
    vmem = pl.BlockSpec(memory_space=pltpu.VMEM)
    return pl.pallas_call(
        coil_kernel,
        in_specs=[vmem] * 8 + [pl.BlockSpec(memory_space=pl.ANY)],
        out_specs=[vmem] * 2,
        out_shape=[
            jax.ShapeDtypeStruct((own * depth, 2 * LANES), jnp.float32),
            jax.ShapeDtypeStruct((own * depth, 2 * LANES), jnp.bfloat16),
        ],
        scratch_shapes=[
            pltpu.VMEM((2, NY * depth, LANES), jnp.float32),
            pltpu.VMEM((2, own * depth, LANES), jnp.float32),
            pltpu.VMEM((depth, NY, 2 * LANES), jnp.bfloat16),
            pltpu.VMEM((count - 1, depth, own, 2 * LANES), jnp.bfloat16),
            pltpu.VMEM((own, depth, 2, BLOCK, LANES), jnp.bfloat16),
            pltpu.VMEM((4, LANES, 8 * BLOCK), jnp.bfloat16),
            pltpu.VMEM((8, own, 8 * BLOCK), jnp.float32),
            pltpu.VMEM((4, own * depth, LANES), jnp.float32),
            pltpu.SemaphoreType.DMA((count - 1, depth)),
            pltpu.SemaphoreType.DMA((count - 1, depth)),
            pltpu.SemaphoreType.DMA,
        ],
        compiler_params=pltpu.CompilerParams(
            collective_id=1, has_side_effects=True, vmem_limit_bytes=48 * 1024 * 1024
        ),
        cost_estimate=pl.CostEstimate(
            flops=coils * 2**31, bytes_accessed=coils * 2**22, transcendentals=0
        ),
    )(
        moved, sens, kspace, mask, row_matrix, row_matrix.T, column_tables, index_rows,
        weights.reshape(own, depth, 2, BLOCK, LANES),
    )


def own_coil_maps(sensitivity):
    coils, row_count, depth, width = sensitivity.shape
    bins, count = lax.axis_size("bin"), lax.axis_size("coil")
    share, held = row_count // bins, coils // count
    me = lax.axis_index("coil")
    first = lax.axis_index("bin") * share
    parts = []
    for step in range(count):
        target = lax.rem(me + step, count)
        part = lax.dynamic_slice(
            sensitivity, (target * held, first, 0, 0), (held, share, depth, width)
        )
        parts.append(shifted(part, "coil", step) if step else part)
    full = lax.all_gather(jnp.stack(parts), "bin", axis=0, tiled=False)
    return full.transpose(2, 4, 1, 0, 3, 5).reshape(held, depth, count, row_count, width)


def one_hot(test):
    return jnp.where(test, 1.0, 0.0).astype(jnp.bfloat16)


def turn(values):
    return pltpu.roll(values, BLOCK, 1)


def strips_to_parts(first, second, low):
    return jnp.where(low, first, turn(second)), jnp.where(low, turn(first), second)


def meet(axis):
    me, count = lax.axis_index(axis), lax.axis_size(axis)
    barrier = pltpu.get_barrier_semaphore()
    for step in range(1, count):
        pl.semaphore_signal(
            barrier,
            inc=1,
            device_id={axis: lax.rem(me + step, count)},
            device_id_type=pl.DeviceIdType.MESH,
        )
    pl.semaphore_wait(barrier, count - 1)


def forward_kernel(
    w_hbm, earlier_ref, current_ref, index_ref, out_ref, w_buffer, source_ref,
    load_sem, send_sem, recv_sem,
):
    me, count = lax.axis_index("coil"), lax.axis_size("coil")
    total_rows = current_ref.shape[0]
    bands = total_rows // ROWS
    first_row = me * total_rows

    def load(b):
        return pltpu.make_async_copy(
            w_hbm.at[pl.ds(b * ROWS, ROWS)], w_buffer.at[b % 2], load_sem.at[b % 2]
        )

    load(0).start()
    meet("coil")
    sends = []
    for b in range(bands):
        load(b).wait()
        if b + 1 < bands:
            load(b + 1).start()
        part = pl.ds(b * ROWS, ROWS)
        place = pl.ds(pl.multiple_of(first_row + b * ROWS, ROWS), ROWS)
        forward_band(
            w_buffer.at[b % 2],
            earlier_ref.at[part],
            current_ref.at[part],
            index_ref.at[part],
            out_ref.at[place],
            source_ref,
        )
        for step in range(1, count):
            copy = pltpu.make_async_remote_copy(
                src_ref=out_ref.at[place],
                dst_ref=out_ref.at[place],
                send_sem=send_sem.at[b, step - 1],
                recv_sem=recv_sem.at[b, step - 1],
                device_id={"coil": lax.rem(me + step, count)},
                device_id_type=pl.DeviceIdType.MESH,
            )
            copy.start()
            sends.append(copy)
    for copy in sends:
        copy.wait()


def forward_band(w_ref, earlier_ref, current_ref, index_ref, out_ref, source_ref):
    f32, bf16 = jnp.float32, jnp.bfloat16
    rows = ROWS
    low = lax.broadcasted_iota(jnp.int32, (rows, LANES), 1) < BLOCK
    earlier = earlier_ref[...].astype(f32)
    own = (earlier[:, :LANES], earlier[:, LANES:])
    pieces = jnp.concatenate(strips_to_parts(own[0], own[1], low), axis=0).astype(bf16)
    numbers = lax.broadcasted_iota(jnp.int32, (rows, 2 * rows), 1)
    index = index_ref[...]
    chosen = [
        jnp.dot(one_hot(index[:, s : s + 1] == numbers), pieces, preferred_element_type=f32)
        for s in range(2)
    ]
    other = strips_to_parts(chosen[0], chosen[1], low)
    for k, image in enumerate((own, other)):
        for c in range(2):
            plain, turned = image[c], turn(image[c])
            zero = jnp.zeros_like(plain)
            base = k * 8 + c * 2
            source_ref[base, :, :LANES] = jnp.where(low, plain, 0.0)
            source_ref[base + 1, :, :LANES] = jnp.where(low, 0.0, turned)
            source_ref[base + 4, :, LANES:] = jnp.where(low, turned, 0.0)
            source_ref[base + 5, :, LANES:] = jnp.where(low, 0.0, plain)
            for h in range(2):
                source_ref[base + h, :, LANES:] = zero
                source_ref[base + 4 + h, :, :LANES] = zero

    lane = lax.broadcasted_iota(jnp.int32, (BLOCK, LANES), 1)
    row = lax.broadcasted_iota(jnp.int32, (BLOCK, LANES), 0)
    same_slot = row % 2 == lane // 64
    spot = lane % 8
    er = lax.broadcasted_iota(jnp.int32, (BLOCK, 2 * LANES), 0)
    el = lax.broadcasted_iota(jnp.int32, (BLOCK, 2 * LANES), 1)
    expand = one_hot(el % BLOCK == er // 2 * 2 + el // LANES)
    low8 = low[:8]

    def one_row(y):
        start = pl.multiple_of(y * 8, 8)
        weights = jnp.concatenate(
            [w_ref[pl.ds(start, 8), s].reshape(8 * BLOCK, LANES) for s in range(2)], axis=1
        )
        source = source_ref[:, pl.ds(start, 8), :].reshape(LANES, 2 * LANES).astype(bf16)
        products = lax.dot_general(
            weights, source, (((1,), (1,)), ((), ())), preferred_element_type=f32
        ).reshape(8, BLOCK, LANES)
        kept = products[0]
        for z in range(1, 8):
            kept = jnp.where(spot == z, products[z], kept)
        kept = jnp.where(same_slot, kept, 0.0)
        return kept + turn(kept)

    def two_rows(step):
        at = pl.multiple_of(step * 16, 16)
        pair = jnp.where(lane < BLOCK, one_row(step * 2), one_row(step * 2 + 1))
        spread = jnp.dot(pair.T.astype(bf16), expand, preferred_element_type=f32)
        lines = []
        for y in range(2):
            parts = []
            for c in range(2):
                strips = []
                for s in range(2):
                    i = y * 64 + s * 32 + c * 16
                    strips.append(spread[i : i + 8, :LANES] + spread[i + 8 : i + 16, LANES:])
                parts.append(jnp.where(low8, strips[0], strips[1]))
            lines.append(jnp.concatenate(parts, axis=1))
        warped = jnp.concatenate(lines, axis=0)
        now = current_ref[pl.ds(at, 16), :].astype(f32)
        out_ref[pl.ds(at, 16), :] = (now + warped).astype(bf16)

    def four_rows(step, carry):
        two_rows(step * 2)
        two_rows(step * 2 + 1)
        return carry

    lax.fori_loop(0, rows // 32, four_rows, 0)


def warp_forward(earlier, current, weights, index_columns):
    count = lax.axis_size("coil")
    rows = earlier.shape[0]
    bands = rows // ROWS
    vmem = pl.BlockSpec(memory_space=pltpu.VMEM)
    return pl.pallas_call(
        forward_kernel,
        in_specs=[pl.BlockSpec(memory_space=pl.ANY), vmem, vmem, vmem],
        out_specs=vmem,
        out_shape=jax.ShapeDtypeStruct((count * rows, 2 * LANES), jnp.bfloat16),
        scratch_shapes=[
            pltpu.VMEM((2, ROWS, 2, BLOCK, LANES), jnp.bfloat16),
            pltpu.VMEM((16, ROWS, 2 * LANES), jnp.float32),
            pltpu.SemaphoreType.DMA((2,)),
            pltpu.SemaphoreType.DMA((bands, count - 1)),
            pltpu.SemaphoreType.DMA((bands, count - 1)),
        ],
        compiler_params=pltpu.CompilerParams(
            collective_id=0, has_side_effects=True, vmem_limit_bytes=40 * 1024 * 1024
        ),
        cost_estimate=pl.CostEstimate(
            flops=bands * 2**31, bytes_accessed=bands * 2**22, transcendentals=0
        ),
    )(weights, earlier, current, index_columns)


def arrange_weights(blocks):
    count = blocks.shape[0]
    lines = blocks.reshape(count, 2, BLOCK * BLOCK // LANES, LANES)
    return lines.transpose(0, 2, 1, 3).reshape(count // 2, 2, BLOCK, LANES)


def band_places(block_index):
    in_band = block_index[:, 1] % (2 * ROWS)
    return (in_band % 2 * ROWS + in_band // 2).reshape(-1, 2)


def on_device(cine_image, warp_blocks, warp_index, sample_mask, kspace_data, sensitivity):
    current = cine_image[0]
    row_count, depth_count, full_width = current.shape
    row_matrix = make_row_matrix(NX)
    column_tables = make_column_tables(NY).reshape(2 * NY, NY)
    earlier = shifted(cine_image, "bin", 1)[0]
    sens = own_coil_maps(sensitivity)
    kspace = kspace_data[0].transpose(0, 2, 1, 3)
    weights = arrange_weights(warp_blocks[0])
    places = band_places(warp_index[0])
    flat_shape = (row_count * depth_count, full_width)
    moved_image = warp_forward(
        earlier.reshape(flat_shape), current.reshape(flat_shape), weights, places
    )
    data_grad, pulled = coil_gradient(
        moved_image, sens, kspace, sample_mask[0], row_matrix, column_tables, places.T, weights
    )
    pulled = pulled.reshape(current.shape)
    from_next = shifted(pulled, "bin", -1)
    return (data_grad.reshape(current.shape) + from_next.astype(jnp.float32))[None]


def solution(mesh):
    return jax.shard_map(
        on_device,
        mesh=mesh,
        in_specs=(
            P("bin", "coil", None, None),
            P("bin", "coil", None, None),
            P("bin", "coil", None),
            P("bin", None, None),
            P("bin", "coil", None, None, None),
            P(None, "coil", None, None),
        ),
        out_specs=P("bin", "coil", None, None),
        check_vma=False,
    )
```

```python
import jax
import jax.numpy as jnp
from jax import lax
from jax.experimental import pallas as pl
from jax.experimental.pallas import tpu as pltpu
from jax.sharding import PartitionSpec as P

NY = 256
NX = 128
BLOCK = 64
LANES = 128
ROWS = 128
LAG = 2


def shifted(block, axis, distance):
    devices = range(lax.axis_size(axis))
    route = [((i - distance) % len(devices), i) for i in devices]
    return lax.ppermute(block, axis, route)


def cosine_sine(length):
    positions = jnp.arange(length, dtype=jnp.int32)
    phases = positions[:, None] * positions[None, :] % length
    angles = phases.astype(jnp.float32) * (2.0 * jnp.pi / length)
    factor = 1.0 / jnp.sqrt(jnp.asarray(length, jnp.float32))
    return (jnp.cos(angles) * factor, jnp.sin(angles) * factor)


def make_row_matrix(length):
    cosine_table, sine_table = cosine_sine(length)
    upper_half = jnp.concatenate([cosine_table, -sine_table], axis=1)
    lower_half = jnp.concatenate([sine_table, cosine_table], axis=1)
    return jnp.concatenate([upper_half, lower_half], axis=0).astype(jnp.bfloat16)


def make_column_tables(length):
    cosine_table, sine_table = cosine_sine(length)
    return jnp.stack([cosine_table, sine_table]).astype(jnp.bfloat16)


def halves_swapped(values):
    return jnp.concatenate([values[:, LANES:], values[:, :LANES]], axis=1)


def coil_kernel(
    moved_ref, sens_ref, kspace_ref, mask_ref, row_ref, back_ref, column_ref, index_ref, w_hbm,
    out_ref, pulled_ref,
    wide_ref, sums_ref, send_ref, recv_ref, w_ref, expand_ref, spread_ref, warp_ref,
    send_sem, recv_sem, load_sem,
):
    f32, bf16 = jnp.float32, jnp.bfloat16
    me, count = lax.axis_index("coil"), lax.axis_size("coil")
    coils, depth = sens_ref.shape[0], sens_ref.shape[1]
    own = NY // count
    load = pltpu.make_async_copy(w_hbm, w_ref, load_sem)
    load.start()
    meet(peers_of("coil"))
    er = lax.broadcasted_iota(jnp.int32, (LANES, 8 * BLOCK), 0)
    el = lax.broadcasted_iota(jnp.int32, (LANES, 8 * BLOCK), 1)
    for s in range(2):
        for h in range(2):
            expand_ref[s * 2 + h] = one_hot(er == s * BLOCK + el % BLOCK // 2 * 2 + h)
    mr = lax.broadcasted_iota(jnp.int32, (8, 8 * BLOCK), 0)
    ml = lax.broadcasted_iota(jnp.int32, (8, 8 * BLOCK), 1)
    masks = [(ml // BLOCK == mr) & (ml % 2 == k) for k in range(2)]
    low = lax.broadcasted_iota(jnp.int32, (ROWS, LANES), 1) < BLOCK
    low8 = low[:8]
    for part in range(2):
        wide_ref[part] = moved_ref[:, part * LANES : (part + 1) * LANES].astype(f32)

    def multiply(left, right):
        return jnp.dot(left, right, preferred_element_type=f32)

    def transfer(step, z):
        target = lax.rem(me + step, count)
        rows = pl.ds(pl.multiple_of(target * own, own), own)
        return pltpu.make_async_remote_copy(
            src_ref=send_ref.at[z, rows],
            dst_ref=recv_ref.at[step - 1, z],
            send_sem=send_sem.at[step - 1, z],
            recv_sem=recv_sem.at[step - 1, z],
            device_id={"coil": target},
            device_id_type=pl.DeviceIdType.MESH,
        )

    def one_depth(z):
        image_re = wide_ref[0, pl.ds(z, NY, stride=depth), :]
        image_im = wide_ref[1, pl.ds(z, NY, stride=depth), :]
        mask = mask_ref[...].astype(f32)
        mask = jnp.concatenate([mask, mask], axis=1)
        total_re = total_im = 0.0
        for c in range(coils):
            sens = jnp.concatenate(
                [sens_ref[c, z, lax.rem(me - w + count, count)] for w in range(count)], axis=0
            ).astype(f32)
            sens_re, sens_im = sens[:, :LANES], sens[:, LANES:]
            coil_image = jnp.concatenate(
                [
                    sens_re * image_re - sens_im * image_im,
                    sens_re * image_im + sens_im * image_re,
                ],
                axis=1,
            ).astype(bf16)
            row_spectra = multiply(coil_image, row_ref[...]).astype(bf16)
            products = multiply(column_ref[...], row_spectra)
            direct, turned = products[:NY], halves_swapped(products[NY:])
            spectra = jnp.concatenate(
                [direct[:, :LANES] + turned[:, :LANES], direct[:, LANES:] - turned[:, LANES:]],
                axis=1,
            )
            residual = (mask * (spectra - kspace_ref[c, z].astype(f32))).astype(bf16)
            products = multiply(column_ref[...], residual)
            direct, turned = products[:NY], halves_swapped(products[NY:])
            columns = jnp.concatenate(
                [direct[:, :LANES] - turned[:, :LANES], direct[:, LANES:] + turned[:, LANES:]],
                axis=1,
            ).astype(bf16)
            back = multiply(columns, back_ref[...])
            back_re, back_im = back[:, :LANES], back[:, LANES:]
            total_re += sens_re * back_re + sens_im * back_im
            total_im += sens_re * back_im - sens_im * back_re
        send_ref[z] = jnp.concatenate([total_re, total_im], axis=1).astype(bf16)
        for step in range(1, count):
            transfer(step, z).start()

    def adjoint_depth(z):
        rows = pl.ds(pl.multiple_of(me * own, own), own)
        total = send_ref[z, rows, :].astype(f32)
        for step in range(1, count):
            transfer(step, z).wait_recv()
            total += recv_ref[step - 1, z].astype(f32)
        for part in range(2):
            sums_ref[part, pl.ds(z, own, stride=depth), :] = total[
                :, part * LANES : (part + 1) * LANES
            ]
        grad = total.astype(bf16)
        for s in range(2):
            for h in range(2):
                for c in range(2):
                    spread_ref[s * 4 + c * 2 + h] = multiply(
                        grad[:, c * LANES : (c + 1) * LANES], expand_ref[s * 2 + h]
                    )

        def one_group(q):
            start = pl.multiple_of(q * 8, 8)
            tiles = []
            for s in range(2):
                values = [spread_ref[s * 4 + ch, pl.ds(start, 8), :] for ch in range(4)]
                left = jnp.concatenate(
                    [jnp.where(masks[k], values[ch], 0.0) for k in range(2) for ch in range(4)],
                    axis=0,
                ).astype(bf16)
                weights = w_ref[pl.ds(start, 8), z, s].reshape(8 * BLOCK, LANES)
                tiles.append(multiply(left, weights))
            for k in range(2):
                for c in range(2):
                    at = k * 32 + c * 16
                    plain = jnp.where(low8, tiles[0][at : at + 8], tiles[1][at + 8 : at + 16])
                    moved = jnp.where(low8, tiles[1][at : at + 8], tiles[0][at + 8 : at + 16])
                    place = pl.ds(start * depth + z, 8, stride=depth)
                    warp_ref[k * 2 + c, place, :] = plain + turn(moved)

        together = min(4, own // 8)

        def some_groups(step, carry):
            for i in range(together):
                one_group(step * together + i)
            return carry

        lax.fori_loop(0, own // 8 // together, some_groups, 0)

    def forward_step(z, carry):
        one_depth(z)

        @pl.when(z >= LAG)
        def _():
            @pl.when(z == LAG)
            def _():
                load.wait()

            adjoint_depth(z - LAG)

        return carry

    def last_step(z, carry):
        adjoint_depth(z)
        return carry

    def sent(z, carry):
        for step in range(1, count):
            transfer(step, z).wait_send()
        return carry

    lax.fori_loop(0, depth, forward_step, 0)
    lax.fori_loop(depth - LAG, depth, last_step, 0)
    out_ref[...] = jnp.concatenate([sums_ref[0], sums_ref[1]], axis=1)
    numbers = lax.broadcasted_iota(jnp.int32, (2 * ROWS, ROWS), 0)
    for band in range(own * depth // ROWS):
        part = pl.ds(band * ROWS, ROWS)
        index = index_ref[:, part]
        select = jnp.concatenate(
            [one_hot(index[s : s + 1, :] == numbers) for s in range(2)], axis=1
        )
        terms = jnp.concatenate(
            strips_to_parts(warp_ref[2, part, :], warp_ref[3, part, :], low), axis=0
        )
        upper = terms.astype(bf16)
        lower = (terms - upper.astype(f32)).astype(bf16)
        summed = multiply(select, upper) + multiply(select, lower)
        parts = strips_to_parts(summed[:ROWS], summed[ROWS:], low)
        pulled_ref[part, :] = jnp.concatenate(
            [parts[0] + warp_ref[0, part, :], parts[1] + warp_ref[1, part, :]], axis=1
        ).astype(bf16)
    lax.fori_loop(0, depth, sent, 0)


def coil_gradient(
    moved, sens, kspace, mask, row_matrix, column_tables, index_rows, weights
):
    count = lax.axis_size("coil")
    coils, depth = sens.shape[:2]
    own = NY // count
    vmem = pl.BlockSpec(memory_space=pltpu.VMEM)
    return pl.pallas_call(
        coil_kernel,
        in_specs=[vmem] * 8 + [pl.BlockSpec(memory_space=pl.ANY)],
        out_specs=[vmem] * 2,
        out_shape=[
            jax.ShapeDtypeStruct((own * depth, 2 * LANES), jnp.float32),
            jax.ShapeDtypeStruct((own * depth, 2 * LANES), jnp.bfloat16),
        ],
        scratch_shapes=[
            pltpu.VMEM((2, NY * depth, LANES), jnp.float32),
            pltpu.VMEM((2, own * depth, LANES), jnp.float32),
            pltpu.VMEM((depth, NY, 2 * LANES), jnp.bfloat16),
            pltpu.VMEM((count - 1, depth, own, 2 * LANES), jnp.bfloat16),
            pltpu.VMEM((own, depth, 2, BLOCK, LANES), jnp.bfloat16),
            pltpu.VMEM((4, LANES, 8 * BLOCK), jnp.bfloat16),
            pltpu.VMEM((8, own, 8 * BLOCK), jnp.float32),
            pltpu.VMEM((4, own * depth, LANES), jnp.float32),
            pltpu.SemaphoreType.DMA((count - 1, depth)),
            pltpu.SemaphoreType.DMA((count - 1, depth)),
            pltpu.SemaphoreType.DMA,
        ],
        compiler_params=pltpu.CompilerParams(
            collective_id=1, has_side_effects=True, vmem_limit_bytes=48 * 1024 * 1024
        ),
        cost_estimate=pl.CostEstimate(
            flops=coils * 2**31, bytes_accessed=coils * 2**22, transcendentals=0
        ),
    )(
        moved, sens, kspace, mask, row_matrix, row_matrix.T, column_tables, index_rows,
        weights.reshape(own, depth, 2, BLOCK, LANES),
    )


def arrange_maps(maps):
    bins, count, held, share, depth, width = maps.shape
    return maps.transpose(2, 4, 1, 0, 3, 5).reshape(held, depth, count, bins * share, width)


def one_hot(test):
    return jnp.where(test, 1.0, 0.0).astype(jnp.bfloat16)


def turn(values):
    return pltpu.roll(values, BLOCK, 1)


def strips_to_parts(first, second, low):
    return jnp.where(low, first, turn(second)), jnp.where(low, turn(first), second)


def peers_of(axis):
    me, count = lax.axis_index(axis), lax.axis_size(axis)
    return [{axis: lax.rem(me + step, count)} for step in range(1, count)]


def meet(peers):
    barrier = pltpu.get_barrier_semaphore()
    for peer in peers:
        pl.semaphore_signal(
            barrier, inc=1, device_id=peer, device_id_type=pl.DeviceIdType.MESH
        )
    pl.semaphore_wait(barrier, len(peers))


def forward_kernel(
    w_hbm, sens_hbm, earlier_ref, current_ref, index_ref, out_ref, maps_ref,
    w_buffer, source_ref, load_sem, send_sem, recv_sem,
    own_sem, coil_send, coil_recv, bin_send, bin_recv,
):
    me, count = lax.axis_index("coil"), lax.axis_size("coil")
    total_rows = current_ref.shape[0]
    bands = total_rows // ROWS
    first_row = me * total_rows

    def load(b):
        return pltpu.make_async_copy(
            w_hbm.at[pl.ds(b * ROWS, ROWS)], w_buffer.at[b % 2], load_sem.at[b % 2]
        )

    my_bin = lax.axis_index("bin")
    held, share = maps_ref.shape[2:4]

    def coil_part(target):
        return sens_hbm.at[pl.ds(target * held, held), pl.ds(my_bin * share, share)]

    load(0).start()
    own_maps = pltpu.make_async_copy(coil_part(me), maps_ref.at[my_bin, 0], own_sem)
    own_maps.start()
    meet(peers_of("coil") + peers_of("bin"))
    swaps = []
    for step in range(1, count):
        target = lax.rem(me + step, count)
        swaps.append(
            pltpu.make_async_remote_copy(
                src_ref=coil_part(target),
                dst_ref=maps_ref.at[my_bin, step],
                send_sem=coil_send.at[step - 1],
                recv_sem=coil_recv.at[step - 1],
                device_id={"coil": target},
                device_id_type=pl.DeviceIdType.MESH,
            )
        )
        swaps[-1].start()
    sends = []
    for b in range(bands):
        load(b).wait()
        if b + 1 < bands:
            load(b + 1).start()
        part = pl.ds(b * ROWS, ROWS)
        place = pl.ds(pl.multiple_of(first_row + b * ROWS, ROWS), ROWS)
        forward_band(
            w_buffer.at[b % 2],
            earlier_ref.at[part],
            current_ref.at[part],
            index_ref.at[part],
            out_ref.at[place],
            source_ref,
        )
        for step in range(1, count):
            copy = pltpu.make_async_remote_copy(
                src_ref=out_ref.at[place],
                dst_ref=out_ref.at[place],
                send_sem=send_sem.at[b, step - 1],
                recv_sem=recv_sem.at[b, step - 1],
                device_id={"coil": lax.rem(me + step, count)},
                device_id_type=pl.DeviceIdType.MESH,
            )
            copy.start()
            sends.append(copy)
        if b == 0:
            own_maps.wait()
            for copy in swaps:
                copy.wait()
            for step, peer in enumerate(peers_of("bin")):
                copy = pltpu.make_async_remote_copy(
                    src_ref=maps_ref.at[my_bin],
                    dst_ref=maps_ref.at[my_bin],
                    send_sem=bin_send.at[step],
                    recv_sem=bin_recv.at[step],
                    device_id=peer,
                    device_id_type=pl.DeviceIdType.MESH,
                )
                copy.start()
                sends.append(copy)
    for copy in sends:
        copy.wait()


def forward_band(w_ref, earlier_ref, current_ref, index_ref, out_ref, source_ref):
    f32, bf16 = jnp.float32, jnp.bfloat16
    rows = ROWS
    low = lax.broadcasted_iota(jnp.int32, (rows, LANES), 1) < BLOCK
    earlier = earlier_ref[...].astype(f32)
    own = (earlier[:, :LANES], earlier[:, LANES:])
    pieces = jnp.concatenate(strips_to_parts(own[0], own[1], low), axis=0).astype(bf16)
    numbers = lax.broadcasted_iota(jnp.int32, (rows, 2 * rows), 1)
    index = index_ref[...]
    chosen = [
        jnp.dot(one_hot(index[:, s : s + 1] == numbers), pieces, preferred_element_type=f32)
        for s in range(2)
    ]
    other = strips_to_parts(chosen[0], chosen[1], low)
    for k, image in enumerate((own, other)):
        for c in range(2):
            plain, turned = image[c], turn(image[c])
            zero = jnp.zeros_like(plain)
            base = k * 8 + c * 2
            source_ref[base, :, :LANES] = jnp.where(low, plain, 0.0)
            source_ref[base + 1, :, :LANES] = jnp.where(low, 0.0, turned)
            source_ref[base + 4, :, LANES:] = jnp.where(low, turned, 0.0)
            source_ref[base + 5, :, LANES:] = jnp.where(low, 0.0, plain)
            for h in range(2):
                source_ref[base + h, :, LANES:] = zero
                source_ref[base + 4 + h, :, :LANES] = zero

    lane = lax.broadcasted_iota(jnp.int32, (BLOCK, LANES), 1)
    row = lax.broadcasted_iota(jnp.int32, (BLOCK, LANES), 0)
    same_slot = row % 2 == lane // 64
    spot = lane % 8
    er = lax.broadcasted_iota(jnp.int32, (BLOCK, 2 * LANES), 0)
    el = lax.broadcasted_iota(jnp.int32, (BLOCK, 2 * LANES), 1)
    expand = one_hot(el % BLOCK == er // 2 * 2 + el // LANES)
    low8 = low[:8]

    def one_row(y):
        start = pl.multiple_of(y * 8, 8)
        weights = jnp.concatenate(
            [w_ref[pl.ds(start, 8), s].reshape(8 * BLOCK, LANES) for s in range(2)], axis=1
        )
        source = source_ref[:, pl.ds(start, 8), :].reshape(LANES, 2 * LANES).astype(bf16)
        products = lax.dot_general(
            weights, source, (((1,), (1,)), ((), ())), preferred_element_type=f32
        ).reshape(8, BLOCK, LANES)
        kept = products[0]
        for z in range(1, 8):
            kept = jnp.where(spot == z, products[z], kept)
        kept = jnp.where(same_slot, kept, 0.0)
        return kept + turn(kept)

    def two_rows(step):
        at = pl.multiple_of(step * 16, 16)
        pair = jnp.where(lane < BLOCK, one_row(step * 2), one_row(step * 2 + 1))
        spread = jnp.dot(pair.T.astype(bf16), expand, preferred_element_type=f32)
        lines = []
        for y in range(2):
            parts = []
            for c in range(2):
                strips = []
                for s in range(2):
                    i = y * 64 + s * 32 + c * 16
                    strips.append(spread[i : i + 8, :LANES] + spread[i + 8 : i + 16, LANES:])
                parts.append(jnp.where(low8, strips[0], strips[1]))
            lines.append(jnp.concatenate(parts, axis=1))
        warped = jnp.concatenate(lines, axis=0)
        now = current_ref[pl.ds(at, 16), :].astype(f32)
        out_ref[pl.ds(at, 16), :] = (now + warped).astype(bf16)

    def four_rows(step, carry):
        two_rows(step * 2)
        two_rows(step * 2 + 1)
        return carry

    lax.fori_loop(0, rows // 32, four_rows, 0)


def warp_forward(earlier, current, weights, index_columns, sensitivity):
    count, bins = lax.axis_size("coil"), lax.axis_size("bin")
    coils, row_count, depth, width = sensitivity.shape
    held, share = coils // count, row_count // bins
    rows = earlier.shape[0]
    bands = rows // ROWS
    vmem = pl.BlockSpec(memory_space=pltpu.VMEM)
    return pl.pallas_call(
        forward_kernel,
        in_specs=[pl.BlockSpec(memory_space=pl.ANY)] * 2 + [vmem] * 3,
        out_specs=[vmem] * 2,
        out_shape=[
            jax.ShapeDtypeStruct((count * rows, 2 * LANES), jnp.bfloat16),
            jax.ShapeDtypeStruct((bins, count, held, share, depth, width), jnp.bfloat16),
        ],
        scratch_shapes=[
            pltpu.VMEM((2, ROWS, 2, BLOCK, LANES), jnp.bfloat16),
            pltpu.VMEM((16, ROWS, 2 * LANES), jnp.float32),
            pltpu.SemaphoreType.DMA((2,)),
            pltpu.SemaphoreType.DMA((bands, count - 1)),
            pltpu.SemaphoreType.DMA((bands, count - 1)),
            pltpu.SemaphoreType.DMA,
            pltpu.SemaphoreType.DMA((count - 1,)),
            pltpu.SemaphoreType.DMA((count - 1,)),
            pltpu.SemaphoreType.DMA((bins - 1,)),
            pltpu.SemaphoreType.DMA((bins - 1,)),
        ],
        compiler_params=pltpu.CompilerParams(
            collective_id=0, has_side_effects=True, vmem_limit_bytes=40 * 1024 * 1024
        ),
        cost_estimate=pl.CostEstimate(
            flops=bands * 2**31, bytes_accessed=bands * 2**22, transcendentals=0
        ),
    )(weights, sensitivity, earlier, current, index_columns)


def arrange_weights(blocks):
    count = blocks.shape[0]
    lines = blocks.reshape(count, 2, BLOCK * BLOCK // LANES, LANES)
    return lines.transpose(0, 2, 1, 3).reshape(count // 2, 2, BLOCK, LANES)


def band_places(block_index):
    in_band = block_index[:, 1] % (2 * ROWS)
    return (in_band % 2 * ROWS + in_band // 2).reshape(-1, 2)


def on_device(cine_image, warp_blocks, warp_index, sample_mask, kspace_data, sensitivity):
    current = cine_image[0]
    row_count, depth_count, full_width = current.shape
    row_matrix = make_row_matrix(NX)
    column_tables = make_column_tables(NY).reshape(2 * NY, NY)
    earlier = shifted(cine_image, "bin", 1)[0]
    kspace = kspace_data[0].transpose(0, 2, 1, 3)
    weights = arrange_weights(warp_blocks[0])
    places = band_places(warp_index[0])
    flat_shape = (row_count * depth_count, full_width)
    moved_image, maps = warp_forward(
        earlier.reshape(flat_shape), current.reshape(flat_shape), weights, places, sensitivity
    )
    sens = arrange_maps(maps)
    data_grad, pulled = coil_gradient(
        moved_image, sens, kspace, sample_mask[0], row_matrix, column_tables, places.T, weights
    )
    pulled = pulled.reshape(current.shape)
    from_next = shifted(pulled, "bin", -1)
    return (data_grad.reshape(current.shape) + from_next.astype(jnp.float32))[None]


def solution(mesh):
    return jax.shard_map(
        on_device,
        mesh=mesh,
        in_specs=(
            P("bin", "coil", None, None),
            P("bin", "coil", None, None),
            P("bin", "coil", None),
            P("bin", None, None),
            P("bin", "coil", None, None, None),
            P(None, "coil", None, None),
        ),
        out_specs=P("bin", "coil", None, None),
        check_vma=False,
    )
```

```python
import jax
import jax.numpy as jnp
from jax import lax
from jax.experimental import pallas as pl
from jax.experimental.pallas import tpu as pltpu
from jax.sharding import PartitionSpec as P

NY = 256
NX = 128
BLOCK = 64
LANES = 128
ROWS = 128
LAG = 2


def shifted(block, axis, distance):
    devices = range(lax.axis_size(axis))
    route = [((i - distance) % len(devices), i) for i in devices]
    return lax.ppermute(block, axis, route)


def cosine_sine(length):
    positions = jnp.arange(length, dtype=jnp.int32)
    phases = positions[:, None] * positions[None, :] % length
    angles = phases.astype(jnp.float32) * (2.0 * jnp.pi / length)
    factor = 1.0 / jnp.sqrt(jnp.asarray(length, jnp.float32))
    return (jnp.cos(angles) * factor, jnp.sin(angles) * factor)


def make_row_matrix(length):
    cosine_table, sine_table = cosine_sine(length)
    upper_half = jnp.concatenate([cosine_table, -sine_table], axis=1)
    lower_half = jnp.concatenate([sine_table, cosine_table], axis=1)
    return jnp.concatenate([upper_half, lower_half], axis=0).astype(jnp.bfloat16)


def make_column_tables(length):
    cosine_table, sine_table = cosine_sine(length)
    return jnp.stack([cosine_table, sine_table]).astype(jnp.bfloat16)


def halves_swapped(values):
    return jnp.concatenate([values[:, LANES:], values[:, :LANES]], axis=1)


def coil_kernel(
    moved_ref, sens_ref, kspace_ref, mask_ref, row_ref, back_ref, column_ref, index_ref, w_hbm,
    out_ref, pulled_ref,
    wide_ref, sums_ref, send_ref, recv_ref, w_ref, expand_ref, spread_ref, warp_ref,
    send_sem, recv_sem, load_sem,
):
    f32, bf16 = jnp.float32, jnp.bfloat16
    me, count = lax.axis_index("coil"), lax.axis_size("coil")
    coils, depth = sens_ref.shape[0], sens_ref.shape[1]
    own = NY // count
    load = pltpu.make_async_copy(w_hbm, w_ref, load_sem)
    load.start()
    meet(peers_of("coil"))
    er = lax.broadcasted_iota(jnp.int32, (LANES, 8 * BLOCK), 0)
    el = lax.broadcasted_iota(jnp.int32, (LANES, 8 * BLOCK), 1)
    for s in range(2):
        for h in range(2):
            expand_ref[s * 2 + h] = one_hot(er == s * BLOCK + el % BLOCK // 2 * 2 + h)
    mr = lax.broadcasted_iota(jnp.int32, (8, 8 * BLOCK), 0)
    ml = lax.broadcasted_iota(jnp.int32, (8, 8 * BLOCK), 1)
    masks = [(ml // BLOCK == mr) & (ml % 2 == k) for k in range(2)]
    low = lax.broadcasted_iota(jnp.int32, (ROWS, LANES), 1) < BLOCK
    low8 = low[:8]
    for part in range(2):
        wide_ref[part] = moved_ref[:, part * LANES : (part + 1) * LANES].astype(f32)

    def multiply(left, right):
        return jnp.dot(left, right, preferred_element_type=f32)

    def transfer(step, z):
        target = lax.rem(me + step, count)
        rows = pl.ds(pl.multiple_of(target * own, own), own)
        return pltpu.make_async_remote_copy(
            src_ref=send_ref.at[z, rows],
            dst_ref=recv_ref.at[step - 1, z],
            send_sem=send_sem.at[step - 1, z],
            recv_sem=recv_sem.at[step - 1, z],
            device_id={"coil": target},
            device_id_type=pl.DeviceIdType.MESH,
        )

    def one_depth(z):
        image_re = wide_ref[0, pl.ds(z, NY, stride=depth), :]
        image_im = wide_ref[1, pl.ds(z, NY, stride=depth), :]
        mask = mask_ref[...].astype(f32)
        mask = jnp.concatenate([mask, mask], axis=1)
        total_re = total_im = 0.0
        for c in range(coils):
            sens = jnp.concatenate(
                [sens_ref[c, z, lax.rem(me - w + count, count)] for w in range(count)], axis=0
            ).astype(f32)
            sens_re, sens_im = sens[:, :LANES], sens[:, LANES:]
            coil_image = jnp.concatenate(
                [
                    sens_re * image_re - sens_im * image_im,
                    sens_re * image_im + sens_im * image_re,
                ],
                axis=1,
            ).astype(bf16)
            row_spectra = multiply(coil_image, row_ref[...]).astype(bf16)
            products = multiply(column_ref[...], row_spectra)
            direct, turned = products[:NY], halves_swapped(products[NY:])
            spectra = jnp.concatenate(
                [direct[:, :LANES] + turned[:, :LANES], direct[:, LANES:] - turned[:, LANES:]],
                axis=1,
            )
            residual = (mask * (spectra - kspace_ref[c, z].astype(f32))).astype(bf16)
            products = multiply(column_ref[...], residual)
            direct, turned = products[:NY], halves_swapped(products[NY:])
            columns = jnp.concatenate(
                [direct[:, :LANES] - turned[:, :LANES], direct[:, LANES:] + turned[:, LANES:]],
                axis=1,
            ).astype(bf16)
            back = multiply(columns, back_ref[...])
            back_re, back_im = back[:, :LANES], back[:, LANES:]
            total_re += sens_re * back_re + sens_im * back_im
            total_im += sens_re * back_im - sens_im * back_re
        send_ref[z] = jnp.concatenate([total_re, total_im], axis=1).astype(bf16)
        for step in range(1, count):
            transfer(step, z).start()

    def adjoint_depth(z):
        rows = pl.ds(pl.multiple_of(me * own, own), own)
        total = send_ref[z, rows, :].astype(f32)
        for step in range(1, count):
            transfer(step, z).wait_recv()
            total += recv_ref[step - 1, z].astype(f32)
        for part in range(2):
            sums_ref[part, pl.ds(z, own, stride=depth), :] = total[
                :, part * LANES : (part + 1) * LANES
            ]
        grad = jnp.concatenate([total[:, :LANES], total[:, LANES:]], axis=0).astype(bf16)
        for s in range(2):
            for h in range(2):
                spread = multiply(grad, expand_ref[s * 2 + h])
                for c in range(2):
                    spread_ref[s * 4 + c * 2 + h] = spread[c * own : (c + 1) * own]

        def one_group(q):
            start = pl.multiple_of(q * 8, 8)
            left = []
            for s in range(2):
                values = [spread_ref[s * 4 + ch, pl.ds(start, 8), :] for ch in range(4)]
                left += [jnp.where(masks[k], values[ch], 0.0) for k in range(2) for ch in range(4)]
            weights = jnp.concatenate(
                [w_ref[pl.ds(start, 8), z, s].reshape(8 * BLOCK, LANES) for s in range(2)], axis=1
            )
            products = multiply(jnp.concatenate(left, axis=0).astype(bf16), weights)
            tiles = [products[:BLOCK, :LANES], products[BLOCK:, LANES:]]
            for k in range(2):
                for c in range(2):
                    at = k * 32 + c * 16
                    plain = jnp.where(low8, tiles[0][at : at + 8], tiles[1][at + 8 : at + 16])
                    moved = jnp.where(low8, tiles[1][at : at + 8], tiles[0][at + 8 : at + 16])
                    place = pl.ds(start * depth + z, 8, stride=depth)
                    warp_ref[k * 2 + c, place, :] = plain + turn(moved)

        together = min(4, own // 8)

        def some_groups(step, carry):
            for i in range(together):
                one_group(step * together + i)
            return carry

        lax.fori_loop(0, own // 8 // together, some_groups, 0)

    def forward_step(z, carry):
        one_depth(z)

        @pl.when(z >= LAG)
        def _():
            @pl.when(z == LAG)
            def _():
                load.wait()

            adjoint_depth(z - LAG)

        return carry

    def last_step(z, carry):
        adjoint_depth(z)
        return carry

    def sent(z, carry):
        for step in range(1, count):
            transfer(step, z).wait_send()
        return carry

    lax.fori_loop(0, depth, forward_step, 0)
    lax.fori_loop(depth - LAG, depth, last_step, 0)
    out_ref[...] = jnp.concatenate([sums_ref[0], sums_ref[1]], axis=1)
    numbers = lax.broadcasted_iota(jnp.int32, (2 * ROWS, ROWS), 0)
    for band in range(own * depth // ROWS):
        part = pl.ds(band * ROWS, ROWS)
        index = index_ref[:, part]
        select = jnp.concatenate(
            [one_hot(index[s : s + 1, :] == numbers) for s in range(2)], axis=1
        )
        terms = jnp.concatenate(
            strips_to_parts(warp_ref[2, part, :], warp_ref[3, part, :], low), axis=0
        )
        upper = terms.astype(bf16)
        lower = (terms - upper.astype(f32)).astype(bf16)
        summed = multiply(select, upper) + multiply(select, lower)
        parts = strips_to_parts(summed[:ROWS], summed[ROWS:], low)
        pulled_ref[part, :] = jnp.concatenate(
            [parts[0] + warp_ref[0, part, :], parts[1] + warp_ref[1, part, :]], axis=1
        ).astype(bf16)
    lax.fori_loop(0, depth, sent, 0)


def coil_gradient(
    moved, sens, kspace, mask, row_matrix, column_tables, index_rows, weights
):
    count = lax.axis_size("coil")
    coils, depth = sens.shape[:2]
    own = NY // count
    vmem = pl.BlockSpec(memory_space=pltpu.VMEM)
    return pl.pallas_call(
        coil_kernel,
        in_specs=[vmem] * 8 + [pl.BlockSpec(memory_space=pl.ANY)],
        out_specs=[vmem] * 2,
        out_shape=[
            jax.ShapeDtypeStruct((own * depth, 2 * LANES), jnp.float32),
            jax.ShapeDtypeStruct((own * depth, 2 * LANES), jnp.bfloat16),
        ],
        scratch_shapes=[
            pltpu.VMEM((2, NY * depth, LANES), jnp.float32),
            pltpu.VMEM((2, own * depth, LANES), jnp.float32),
            pltpu.VMEM((depth, NY, 2 * LANES), jnp.bfloat16),
            pltpu.VMEM((count - 1, depth, own, 2 * LANES), jnp.bfloat16),
            pltpu.VMEM((own, depth, 2, BLOCK, LANES), jnp.bfloat16),
            pltpu.VMEM((4, LANES, 8 * BLOCK), jnp.bfloat16),
            pltpu.VMEM((8, own, 8 * BLOCK), jnp.float32),
            pltpu.VMEM((4, own * depth, LANES), jnp.float32),
            pltpu.SemaphoreType.DMA((count - 1, depth)),
            pltpu.SemaphoreType.DMA((count - 1, depth)),
            pltpu.SemaphoreType.DMA,
        ],
        compiler_params=pltpu.CompilerParams(
            collective_id=1, has_side_effects=True, vmem_limit_bytes=48 * 1024 * 1024
        ),
        cost_estimate=pl.CostEstimate(
            flops=coils * 2**31, bytes_accessed=coils * 2**22, transcendentals=0
        ),
    )(
        moved, sens, kspace, mask, row_matrix, row_matrix.T, column_tables, index_rows,
        weights.reshape(own, depth, 2, BLOCK, LANES),
    )


def arrange_maps(maps):
    bins, count, held, share, depth, width = maps.shape
    return maps.transpose(2, 4, 1, 0, 3, 5).reshape(held, depth, count, bins * share, width)


def one_hot(test):
    return jnp.where(test, 1.0, 0.0).astype(jnp.bfloat16)


def turn(values):
    return pltpu.roll(values, BLOCK, 1)


def strips_to_parts(first, second, low):
    return jnp.where(low, first, turn(second)), jnp.where(low, turn(first), second)


def peers_of(axis):
    me, count = lax.axis_index(axis), lax.axis_size(axis)
    return [{axis: lax.rem(me + step, count)} for step in range(1, count)]


def meet(peers):
    barrier = pltpu.get_barrier_semaphore()
    for peer in peers:
        pl.semaphore_signal(
            barrier, inc=1, device_id=peer, device_id_type=pl.DeviceIdType.MESH
        )
    pl.semaphore_wait(barrier, len(peers))


def forward_kernel(
    w_hbm, sens_hbm, earlier_ref, current_ref, index_ref, out_ref, maps_ref,
    w_buffer, source_ref, load_sem, send_sem, recv_sem,
    own_sem, coil_send, coil_recv, bin_send, bin_recv,
):
    me, count = lax.axis_index("coil"), lax.axis_size("coil")
    total_rows = current_ref.shape[0]
    bands = total_rows // ROWS
    first_row = me * total_rows

    def load(b):
        return pltpu.make_async_copy(
            w_hbm.at[pl.ds(b * ROWS, ROWS)], w_buffer.at[b % 2], load_sem.at[b % 2]
        )

    my_bin = lax.axis_index("bin")
    held, share = maps_ref.shape[2:4]

    def coil_part(target):
        return sens_hbm.at[pl.ds(target * held, held), pl.ds(my_bin * share, share)]

    load(0).start()
    own_maps = pltpu.make_async_copy(coil_part(me), maps_ref.at[my_bin, 0], own_sem)
    own_maps.start()
    meet(peers_of("coil") + peers_of("bin"))
    swaps = []
    for step in range(1, count):
        target = lax.rem(me + step, count)
        swaps.append(
            pltpu.make_async_remote_copy(
                src_ref=coil_part(target),
                dst_ref=maps_ref.at[my_bin, step],
                send_sem=coil_send.at[step - 1],
                recv_sem=coil_recv.at[step - 1],
                device_id={"coil": target},
                device_id_type=pl.DeviceIdType.MESH,
            )
        )
        swaps[-1].start()
    sends = []
    for b in range(bands):
        load(b).wait()
        if b + 1 < bands:
            load(b + 1).start()
        part = pl.ds(b * ROWS, ROWS)
        place = pl.ds(pl.multiple_of(first_row + b * ROWS, ROWS), ROWS)
        forward_band(
            w_buffer.at[b % 2],
            earlier_ref.at[part],
            current_ref.at[part],
            index_ref.at[part],
            out_ref.at[place],
            source_ref,
        )
        for step in range(1, count):
            copy = pltpu.make_async_remote_copy(
                src_ref=out_ref.at[place],
                dst_ref=out_ref.at[place],
                send_sem=send_sem.at[b, step - 1],
                recv_sem=recv_sem.at[b, step - 1],
                device_id={"coil": lax.rem(me + step, count)},
                device_id_type=pl.DeviceIdType.MESH,
            )
            copy.start()
            sends.append(copy)
        if b == 0:
            own_maps.wait()
            for copy in swaps:
                copy.wait()
            for step, peer in enumerate(peers_of("bin")):
                copy = pltpu.make_async_remote_copy(
                    src_ref=maps_ref.at[my_bin],
                    dst_ref=maps_ref.at[my_bin],
                    send_sem=bin_send.at[step],
                    recv_sem=bin_recv.at[step],
                    device_id=peer,
                    device_id_type=pl.DeviceIdType.MESH,
                )
                copy.start()
                sends.append(copy)
    for copy in sends:
        copy.wait()


def forward_band(w_ref, earlier_ref, current_ref, index_ref, out_ref, source_ref):
    f32, bf16 = jnp.float32, jnp.bfloat16
    rows = ROWS
    low = lax.broadcasted_iota(jnp.int32, (rows, LANES), 1) < BLOCK
    earlier = earlier_ref[...].astype(f32)
    own = (earlier[:, :LANES], earlier[:, LANES:])
    pieces = jnp.concatenate(strips_to_parts(own[0], own[1], low), axis=0).astype(bf16)
    numbers = lax.broadcasted_iota(jnp.int32, (rows, 2 * rows), 1)
    index = index_ref[...]
    chosen = [
        jnp.dot(one_hot(index[:, s : s + 1] == numbers), pieces, preferred_element_type=f32)
        for s in range(2)
    ]
    other = strips_to_parts(chosen[0], chosen[1], low)
    for k, image in enumerate((own, other)):
        for c in range(2):
            plain, turned = image[c], turn(image[c])
            zero = jnp.zeros_like(plain)
            base = k * 8 + c * 2
            source_ref[base, :, :LANES] = jnp.where(low, plain, 0.0)
            source_ref[base + 1, :, :LANES] = jnp.where(low, 0.0, turned)
            source_ref[base + 4, :, LANES:] = jnp.where(low, turned, 0.0)
            source_ref[base + 5, :, LANES:] = jnp.where(low, 0.0, plain)
            for h in range(2):
                source_ref[base + h, :, LANES:] = zero
                source_ref[base + 4 + h, :, :LANES] = zero

    lane = lax.broadcasted_iota(jnp.int32, (BLOCK, LANES), 1)
    row = lax.broadcasted_iota(jnp.int32, (BLOCK, LANES), 0)
    same_slot = row % 2 == lane // 64
    spot = lane % 8
    er = lax.broadcasted_iota(jnp.int32, (BLOCK, 2 * LANES), 0)
    el = lax.broadcasted_iota(jnp.int32, (BLOCK, 2 * LANES), 1)
    expand = one_hot(el % BLOCK == er // 2 * 2 + el // LANES)
    low8 = low[:8]

    def one_row(y):
        start = pl.multiple_of(y * 8, 8)
        weights = jnp.concatenate(
            [w_ref[pl.ds(start, 8), s].reshape(8 * BLOCK, LANES) for s in range(2)], axis=1
        )
        source = source_ref[:, pl.ds(start, 8), :].reshape(LANES, 2 * LANES).astype(bf16)
        products = lax.dot_general(
            weights, source, (((1,), (1,)), ((), ())), preferred_element_type=f32
        ).reshape(8, BLOCK, LANES)
        kept = products[0]
        for z in range(1, 8):
            kept = jnp.where(spot == z, products[z], kept)
        kept = jnp.where(same_slot, kept, 0.0)
        return kept + turn(kept)

    def two_rows(step):
        at = pl.multiple_of(step * 16, 16)
        pair = jnp.where(lane < BLOCK, one_row(step * 2), one_row(step * 2 + 1))
        spread = jnp.dot(pair.T.astype(bf16), expand, preferred_element_type=f32)
        lines = []
        for y in range(2):
            parts = []
            for c in range(2):
                strips = []
                for s in range(2):
                    i = y * 64 + s * 32 + c * 16
                    strips.append(spread[i : i + 8, :LANES] + spread[i + 8 : i + 16, LANES:])
                parts.append(jnp.where(low8, strips[0], strips[1]))
            lines.append(jnp.concatenate(parts, axis=1))
        warped = jnp.concatenate(lines, axis=0)
        now = current_ref[pl.ds(at, 16), :].astype(f32)
        out_ref[pl.ds(at, 16), :] = (now + warped).astype(bf16)

    def four_rows(step, carry):
        two_rows(step * 2)
        two_rows(step * 2 + 1)
        return carry

    lax.fori_loop(0, rows // 32, four_rows, 0, unroll=2)


def warp_forward(earlier, current, weights, index_columns, sensitivity):
    count, bins = lax.axis_size("coil"), lax.axis_size("bin")
    coils, row_count, depth, width = sensitivity.shape
    held, share = coils // count, row_count // bins
    rows = earlier.shape[0]
    bands = rows // ROWS
    vmem = pl.BlockSpec(memory_space=pltpu.VMEM)
    return pl.pallas_call(
        forward_kernel,
        in_specs=[pl.BlockSpec(memory_space=pl.ANY)] * 2 + [vmem] * 3,
        out_specs=[vmem] * 2,
        out_shape=[
            jax.ShapeDtypeStruct((count * rows, 2 * LANES), jnp.bfloat16),
            jax.ShapeDtypeStruct((bins, count, held, share, depth, width), jnp.bfloat16),
        ],
        scratch_shapes=[
            pltpu.VMEM((2, ROWS, 2, BLOCK, LANES), jnp.bfloat16),
            pltpu.VMEM((16, ROWS, 2 * LANES), jnp.float32),
            pltpu.SemaphoreType.DMA((2,)),
            pltpu.SemaphoreType.DMA((bands, count - 1)),
            pltpu.SemaphoreType.DMA((bands, count - 1)),
            pltpu.SemaphoreType.DMA,
            pltpu.SemaphoreType.DMA((count - 1,)),
            pltpu.SemaphoreType.DMA((count - 1,)),
            pltpu.SemaphoreType.DMA((bins - 1,)),
            pltpu.SemaphoreType.DMA((bins - 1,)),
        ],
        compiler_params=pltpu.CompilerParams(
            collective_id=0, has_side_effects=True, vmem_limit_bytes=40 * 1024 * 1024
        ),
        cost_estimate=pl.CostEstimate(
            flops=bands * 2**31, bytes_accessed=bands * 2**22, transcendentals=0
        ),
    )(weights, sensitivity, earlier, current, index_columns)


def arrange_weights(blocks):
    count = blocks.shape[0]
    lines = blocks.reshape(count, 2, BLOCK * BLOCK // LANES, LANES)
    return lines.transpose(0, 2, 1, 3).reshape(count // 2, 2, BLOCK, LANES)


def band_places(block_index):
    in_band = block_index[:, 1] % (2 * ROWS)
    return (in_band % 2 * ROWS + in_band // 2).reshape(-1, 2)


def on_device(cine_image, warp_blocks, warp_index, sample_mask, kspace_data, sensitivity):
    current = cine_image[0]
    row_count, depth_count, full_width = current.shape
    row_matrix = make_row_matrix(NX)
    column_tables = make_column_tables(NY).reshape(2 * NY, NY)
    earlier = shifted(cine_image, "bin", 1)[0]
    kspace = kspace_data[0].transpose(0, 2, 1, 3)
    weights = arrange_weights(warp_blocks[0])
    places = band_places(warp_index[0])
    flat_shape = (row_count * depth_count, full_width)
    moved_image, maps = warp_forward(
        earlier.reshape(flat_shape), current.reshape(flat_shape), weights, places, sensitivity
    )
    sens = arrange_maps(maps)
    data_grad, pulled = coil_gradient(
        moved_image, sens, kspace, sample_mask[0], row_matrix, column_tables, places.T, weights
    )
    pulled = pulled.reshape(current.shape)
    from_next = shifted(pulled, "bin", -1)
    return (data_grad.reshape(current.shape) + from_next.astype(jnp.float32))[None]


def solution(mesh):
    return jax.shard_map(
        on_device,
        mesh=mesh,
        in_specs=(
            P("bin", "coil", None, None),
            P("bin", "coil", None, None),
            P("bin", "coil", None),
            P("bin", None, None),
            P("bin", "coil", None, None, None),
            P(None, "coil", None, None),
        ),
        out_specs=P("bin", "coil", None, None),
        check_vma=False,
    )
```
